32 devices in a mesh: section: 4 (over x, core), tensor: 4 (over z), dp: 2 (over y).
Axes of the slice: x: 2, y: 2, z: 4, core: 2. Of those that a mesh axis runs over, the one named last changes fastest.
Arguments:
- act_inbox: bfloat16 [4, 1024, 16384], P('section', 'dp', 'tensor'), may hold values from -6 to 6
- grad_inbox: bfloat16 [4, 1024, 16384], P('section', 'dp', 'tensor'), may hold values from -0.125 to 0.125
- queries: bfloat16 [4, 1024, 16384], P('section', 'dp', 'tensor'), may hold values from -400 to 400
- keys_values: bfloat16 [4, 2, 1024, 1024], P('section', None, 'dp', 'tensor'), may hold values from -6 to 6
- saved_attn: bfloat16 [4, 1024, 16384], P('section', 'dp', 'tensor'), may hold values from -6 to 6
- down_adapt: bfloat16 [4, 8, 16, 16384], P('section', None, None, 'tensor'), may hold values from -0.375 to 0.375
- up_adapt: bfloat16 [4, 8, 16, 16384], P('section', None, None, 'tensor'), may hold values from -0.75 to 0.75
- seg_blocks: int32 [4, 2, 2, 3], P('section', None, 'dp'), may hold values from 1 to 4, 8 in all within a row
- seg_pads: int32 [4, 2, 2, 3], P('section', None, 'dp'), may hold values from 0 to 63
- seg_tenant: int32 [4, 2, 2, 3], P('section', None, 'dp'), may hold values from 0 to 31
- adapter_table: int32 [32], replicated, may hold values from 0 to 7
Outputs:
- new_acts: bfloat16 [4, 1024, 16384], P('section', 'dp', 'tensor')
- grad_down: bfloat16 [4, 8, 16, 16384], P('section', None, None, 'tensor')
- grad_up: bfloat16 [4, 8, 16, 16384], P('section', None, None, 'tensor')
The draws below stay inside these ranges and needn't reach their ends.
Inputs may be any that keep to these rules, and one draw needn't show every extreme that they name: `seg_blocks`: each row of 3 block counts sums to 8.
All inputs are finite; a program needn't handle non-finite values.
Results may differ from the reference program's by a relative error of at most 0.0058.
Values may be sent and summed in bfloat16 or wider, within the bound.
A program may use at most 128 MiB of HBM per device.

```python
import math
import jax
import jax.numpy as jnp
import numpy as np
from jax import lax

HQ = 128
KVH = 8
HD = 128
MODEL_WIDTH = 16384
ADAPTER_RANK = 16
ADAPTER_COUNT = 8
TENANTS = 32
BLOCK = 64
SEGS = 3
TOK_DEV = 512
TOKENS = 1024
N_SECTION = 4
N_DP = 2


def key_field(key):
    return jax.random.truncated_normal(key, -6.0, 6.0, (N_SECTION, TOKENS, KVH * HD), jnp.float32)


def draw_keys_values(key, part):
    key_part = key_field(key)
    key = jax.random.fold_in(key, 3)
    value_part = jax.random.truncated_normal(key, -6.0, 6.0, (N_SECTION, TOKENS, KVH * HD), jnp.float32)
    return jnp.stack([key_part, value_part], axis=1).astype(jnp.bfloat16)


def draw_queries(key, part):
    key = jax.random.fold_in(key, 5)
    first = jax.random.fold_in(key, 0)
    field = jax.random.truncated_normal(first, -6.0, 6.0, (N_SECTION, TOKENS, HQ, HD), jnp.float32)
    return field.reshape(N_SECTION, TOKENS, HQ * HD).astype(jnp.bfloat16)


def touch_ends(drawn, own_key, low, high):
    place = [jax.random.randint(jax.random.fold_in(own_key, axis), (), 0, length) for axis, length in enumerate(drawn.shape)]
    main_axis = drawn.shape.index(max(drawn.shape))
    beside = place[:main_axis] + [(place[main_axis] + 1) % drawn.shape[main_axis]] + place[main_axis + 1:]
    return drawn.at[tuple(place)].set(low).at[tuple(beside)].set(high)


def shard_levels(own_key, shape, cuts, smallest, largest):
    level, own = 1.0, jax.random.fold_in(own_key, 6)
    for dim, shards_of in cuts:
        heights = jnp.exp(jax.random.uniform(jax.random.fold_in(own, dim), (shards_of,), jnp.float32, smallest / len(cuts), largest / len(cuts)))
        level = level * jnp.repeat(heights, shape[dim] // shards_of).reshape([-1 if axis == dim else 1 for axis in range(len(shape))])
    return level


def rank_bounds(amount, lean):
    weights = [(1 << 20) // math.isqrt(standing ** lean) + 1 for standing in range(1, amount + 1)]
    width = 1 + sum(weights) // (1 << 30)
    return np.cumsum(np.array([max(1, weight // width) for weight in weights]))


def skewed_ids(rng, extent, number_of, slope):
    grid = rank_bounds(number_of, slope)
    pick = jax.random.randint(jax.random.fold_in(rng, 1), extent, 0, int(grid[number_of - 1]))
    rank = jnp.searchsorted(jnp.asarray(grid, jnp.int32), pick, side="right")
    return jax.random.permutation(jax.random.fold_in(rng, 2), number_of)[rank].astype(jnp.int32)


def profile(count, total, reach, lean):
    loads = [(1 << 20) // math.isqrt(grade ** lean) + 1 for grade in range(2, count + 1)]
    surplus, counts = total - reach - (count - 1), [1] * (count - 1)
    while surplus > 0:
        candidates = [i for i in range(count - 1) if counts[i] < reach]
        whole, left = sum([loads[i] for i in candidates]), surplus
        for i in candidates:
            extra = min(reach - counts[i], max(1, left * loads[i] // whole), surplus)
            counts[i] = counts[i] + extra
            surplus = surplus - extra
    return np.array([reach] + counts)


def ragged(rng, count, total, most, skew):
    if count == 2:
        one = jax.random.randint(rng, (), max(1, total - most), min(most, total - 1) + 1)
        return jnp.stack([one, total - one])
    tallies = jnp.asarray(profile(count, total, most, skew), jnp.int32)
    couples = (count - 1) // 2
    source_of, receiver = tallies[1:1 + 2 * couples:2], tallies[2:2 + 2 * couples:2]
    slack = jnp.minimum(source_of - 1, most - receiver)
    passed = jax.random.randint(jax.random.fold_in(rng, 1), (couples,), 0, 1 << 20) % (slack + 1)
    tallies = tallies.at[1:1 + 2 * couples:2].set(source_of - passed).at[2:2 + 2 * couples:2].set(receiver + passed)
    return tallies[jax.random.permutation(jax.random.fold_in(rng, 2), count)]


def gaussian(key, dims, scale, limit, shards=(), kind=jnp.bfloat16):
    array = jax.random.normal(key, dims, jnp.float32) * scale
    if len(shards) > 0:
        array = shard_levels(key, dims, shards, -0.22, 0.18) * array
    return jnp.clip(array, min=-limit, max=limit).astype(kind)


def setup_inputs(seed: int = 0) -> dict:
    keys = jax.random.split(jax.random.key(seed), 12)
    return {
        "act_inbox": gaussian(keys[0], (N_SECTION, TOKENS, MODEL_WIDTH), 1.0, 6.0, ((0, 4), (1, 2), (2, 4))),
        "grad_inbox": gaussian(keys[1], (N_SECTION, TOKENS, MODEL_WIDTH), ((TOK_DEV * N_DP) ** -0.5 / 4), 0.125, ((0, 4), (1, 2), (2, 4))),
        "queries": draw_queries(jax.random.fold_in(keys[11], 71), 0),
        "keys_values": draw_keys_values(jax.random.fold_in(keys[11], 71), 0),
        "saved_attn": gaussian(keys[4], (N_SECTION, TOKENS, MODEL_WIDTH), 1.0, 6.0, ((0, 4), (1, 2), (2, 4))),
        "down_adapt": gaussian(keys[5], (N_SECTION, ADAPTER_COUNT, ADAPTER_RANK, MODEL_WIDTH), (MODEL_WIDTH // 64) ** -0.5, 0.375, ((0, 4), (3, 4))),
        "up_adapt": gaussian(keys[6], (N_SECTION, ADAPTER_COUNT, ADAPTER_RANK, MODEL_WIDTH), 64 ** -0.5, 0.75, ((0, 4), (3, 4))),
        "seg_blocks": jax.vmap(lambda own: ragged(own, SEGS, TOK_DEV // BLOCK, TOK_DEV // (2 * BLOCK), 0))(jax.random.split(keys[7], N_SECTION * 2 * N_DP)).reshape((N_SECTION, 2, N_DP, SEGS)).astype(jnp.int32),
        "seg_pads": touch_ends(jax.random.randint(keys[8], (N_SECTION, 2, N_DP, SEGS), 0, BLOCK), jax.random.fold_in(keys[8], 1), 0, BLOCK - 1).astype(jnp.int32),
        "seg_tenant": touch_ends(skewed_ids(keys[9], (N_SECTION, 2, N_DP, SEGS), TENANTS, 2), jax.random.fold_in(keys[9], 3), 0, TENANTS - 1).astype(jnp.int32),
        "adapter_table": touch_ends(jax.random.randint(keys[10], (TENANTS,), 0, ADAPTER_COUNT), jax.random.fold_in(keys[10], 1), 0, ADAPTER_COUNT - 1).astype(jnp.int32),
    }


adapter_scale = 2.0

def token_layout(blocks, padding, tenants, slot_table):
    positions = jnp.arange(TOK_DEV, dtype=jnp.int32)
    seg_ends = jnp.cumsum(blocks).astype(jnp.int32) * BLOCK
    segment = lax.optimization_barrier(jnp.sum((positions[:, None] >= seg_ends[None, :]).astype(jnp.int32), axis=1))
    member = (segment[:, None] == jnp.arange(SEGS, dtype=jnp.int32)[None, :]).astype(jnp.int32)
    live_end = lax.optimization_barrier(jnp.sum(member * (seg_ends - padding)[None, :], axis=1))
    alive = positions < live_end
    tenant_pick = (tenants[:, None] == jnp.arange(TENANTS, dtype=jnp.int32)[None, :]).astype(jnp.int32)
    seg_slot = lax.optimization_barrier(jnp.sum(tenant_pick * slot_table[None, :], axis=1))
    token_slot = lax.optimization_barrier(jnp.sum(member * seg_slot[None, :], axis=1))
    onehot = (token_slot[:, None] == jnp.arange(ADAPTER_COUNT, dtype=jnp.int32)[None, :]).astype(jnp.float32)
    return (segment, alive, onehot)

def attend(queries, keys_values, segment, alive):
    length = queries.shape[0]
    group_size = HQ // KVH
    query_heads = queries.astype(jnp.float32).reshape(length, KVH, group_size, HD)
    key_heads = keys_values[0].astype(jnp.float32).reshape(length, KVH, HD)
    value_heads = keys_values[1].astype(jnp.float32).reshape(length, KVH, HD)
    block_rows = length if length <= 1024 else 512
    positions = jnp.arange(length, dtype=jnp.int32)
    inv_root = 1.0 / math.sqrt(HD)

    def one_block(block_index):
        block_start = block_index * block_rows
        block_q = lax.dynamic_slice_in_dim(query_heads, block_start, block_rows, 0)
        block_pos = block_start + jnp.arange(block_rows, dtype=jnp.int32)
        block_seg = lax.dynamic_slice_in_dim(segment, block_start, block_rows, 0)
        block_live = lax.dynamic_slice_in_dim(alive, block_start, block_rows, 0)
        scores = jnp.einsum('qhgd,khd->hgqk', block_q, key_heads) * inv_root
        allowed = (block_seg[:, None] == segment[None, :]) & (block_pos[:, None] >= positions[None, :])
        allowed = allowed & alive[None, :] & block_live[:, None]
        masked_scores = jnp.where(allowed, scores, -1e+30)
        row_top = lax.optimization_barrier(jnp.max(masked_scores, axis=-1, keepdims=True))
        exponent = jnp.where(allowed, jnp.exp(masked_scores - row_top), 0.0)
        row_total = lax.optimization_barrier(jnp.sum(exponent, axis=-1, keepdims=True))
        row_total = jnp.where(block_live[None, None, :, None], row_total, 1.0)
        weights = (exponent / row_total).astype(jnp.bfloat16)
        attended = jnp.einsum('hgqk,khd->qhgd', weights.astype(jnp.float32), value_heads)
        return attended.astype(jnp.bfloat16).reshape(block_rows, HQ * HD)
    blocks_out = lax.map(one_block, jnp.arange(length // block_rows, dtype=jnp.int32))
    return blocks_out.reshape(length, HQ * HD)

def project_rows(left, right):
    return lax.dot_general(left, right, (((1,), (1,)), ((), ())), preferred_element_type=jnp.float32)

def contract(left, right):
    return lax.dot_general(left, right, (((0,), (0,)), ((), ())), preferred_element_type=jnp.float32)

def select_slots(full, onehot):
    return lax.optimization_barrier(jnp.sum(full.reshape(full.shape[0], onehot.shape[1], -1) * onehot[:, :, None], axis=1))

def spread_tokens(ranked, onehot):
    wide = onehot[:, :, None] * ranked.astype(jnp.float32)[:, None, :]
    return wide.reshape(ranked.shape[0], -1).astype(jnp.bfloat16)

def reference(act_inbox, grad_inbox, queries, keys_values, saved_attn, down_adapt, up_adapt, seg_blocks, seg_pads, seg_tenant, adapter_table):
    received_input = jnp.roll(act_inbox, 1, axis=0)
    returned = jnp.roll(grad_inbox, -1, axis=0)
    acts_all, downs_all, every_up_weight = ([], [], [])
    for relay_section_index in range(N_SECTION):
        down_rows = down_adapt[relay_section_index].reshape(ADAPTER_COUNT * ADAPTER_RANK, MODEL_WIDTH)
        upward_rows = up_adapt[relay_section_index].reshape(ADAPTER_COUNT * ADAPTER_RANK, MODEL_WIDTH)
        pieces = []
        grad_d = jnp.zeros((ADAPTER_COUNT * ADAPTER_RANK, MODEL_WIDTH), jnp.float32)
        up_gradient = jnp.zeros((ADAPTER_COUNT * ADAPTER_RANK, MODEL_WIDTH), jnp.float32)
        for group_index in range(N_DP):
            starting_row = group_index * TOK_DEV
            ending_row = starting_row + TOK_DEV
            segment, alive, onehot = token_layout(seg_blocks[relay_section_index, 0, group_index], seg_pads[relay_section_index, 0, group_index], seg_tenant[relay_section_index, 0, group_index], adapter_table)
            attended = attend(queries[relay_section_index, starting_row:ending_row], keys_values[relay_section_index, :, starting_row:ending_row], segment, alive)
            fwd_rank = select_slots(project_rows(attended, down_rows), onehot).astype(jnp.bfloat16)
            adapter_update = jnp.dot(spread_tokens(fwd_rank, onehot), upward_rows, preferred_element_type=jnp.float32)
            summed_output = received_input[relay_section_index, starting_row:ending_row].astype(jnp.float32) + adapter_scale * adapter_update
            pieces.append(summed_output.astype(jnp.bfloat16))
            back_seg, back_alive, backward_slot_mask = token_layout(seg_blocks[relay_section_index, 1, group_index], seg_pads[relay_section_index, 1, group_index], seg_tenant[relay_section_index, 1, group_index], adapter_table)
            saved_rows = saved_attn[relay_section_index, starting_row:ending_row]
            masked_scores = returned[relay_section_index, starting_row:ending_row] * back_alive[:, None].astype(jnp.bfloat16)
            back_rank = select_slots(project_rows(saved_rows, down_rows), backward_slot_mask).astype(jnp.bfloat16)
            backward_gradient = (adapter_scale * select_slots(project_rows(masked_scores, upward_rows), backward_slot_mask)).astype(jnp.bfloat16)
            up_gradient = up_gradient + contract(spread_tokens(back_rank, backward_slot_mask), masked_scores)
            grad_d = grad_d + contract(spread_tokens(backward_gradient, backward_slot_mask), saved_rows)
        acts_all.append(jnp.concatenate(pieces, axis=0))
        downs_all.append(grad_d.reshape(ADAPTER_COUNT, ADAPTER_RANK, MODEL_WIDTH).astype(jnp.bfloat16))
        every_up_weight.append((adapter_scale * up_gradient).reshape(ADAPTER_COUNT, ADAPTER_RANK, MODEL_WIDTH).astype(jnp.bfloat16))
    return (jnp.stack(acts_all), jnp.stack(downs_all), jnp.stack(every_up_weight))
```

```python
import functools
import math

import jax
import jax.numpy as jnp
from jax import lax
from jax.experimental import pallas as pl
from jax.experimental.pallas import tpu as pltpu
from jax.sharding import PartitionSpec as P

HD = 128
BLOCK = 64
MAX_SEG = 4 * BLOCK
TILE = 128
SCALE = 2.0
F32 = jnp.float32
BF16 = jnp.bfloat16
VMEM_BYTES = 48 * 1024 * 1024

SMEM = pl.BlockSpec(memory_space=pltpu.SMEM)


def dot(left, right, dims):
    return lax.dot_general(left, right, ((dims[:1], dims[1:]), ((), ())), preferred_element_type=F32)


def seg_bounds(blocks, pads, batch):
    bounds, start = [], 0
    for i in range(blocks.shape[-1]):
        end = start + blocks[0, batch, 0, i] * BLOCK
        bounds.append((start, end, end - pads[0, batch, 0, i]))
        start = end
    return bounds


def seg_slots(tenant, table, batch):
    return [table[tenant[0, batch, 0, i]] for i in range(tenant.shape[-1])]


def by_segment(pos, bounds, values):
    out = jnp.zeros_like(pos) + values[0]
    for (start, _, _), value in zip(bounds[1:], values[1:]):
        out = jnp.where(pos >= start, value, out)
    return out


def select_rows(full, keys, key_row, rank):
    out = jnp.zeros((rank, full.shape[1]), F32)
    for i, key in enumerate(keys):
        out = out + jnp.where(key_row == key, full[i * rank : (i + 1) * rank], 0.0)
    return out


def spread_rows(ranked, keys, key_row):
    return jnp.concatenate([jnp.where(key_row == key, ranked, 0.0) for key in keys], axis=0)


def token_row(length):
    return lax.broadcasted_iota(jnp.int32, (1, length), 1)


def pack_up_kernel(tenant, table, up, out):
    rank = up.shape[2]
    for i, slot in enumerate(seg_slots(tenant, table, 1)):
        out[i * rank : (i + 1) * rank, :] = up[0, slot]


def saved_rank_kernel(blocks, pads, tenant, table, saved, down, out, acc):
    step = pl.program_id(0)
    slots, rank = down.shape[1], down.shape[2]

    @pl.when(step == 0)
    def _():
        acc[...] = jnp.zeros_like(acc)

    acc[...] += dot(saved[0], down[0].reshape(slots * rank, -1), (1, 1))

    @pl.when(step == pl.num_programs(0) - 1)
    def _():
        bounds = seg_bounds(blocks, pads, 1)
        slot_row = by_segment(token_row(acc.shape[0]), bounds, seg_slots(tenant, table, 1))
        out[...] = select_rows(acc[...].T, range(slots), slot_row, rank)


def attend_kernel(blocks, pads, tenant, table, q, kv, down, out, acc, bias, live, v_ones, att):
    step = pl.program_id(0)
    length = q.shape[1]
    heads = q.shape[2] // HD
    slots, rank = down.shape[1], down.shape[2]
    factor = math.log2(math.e) / math.sqrt(HD)

    def window(tile):
        first = max(0, tile * TILE - MAX_SEG)
        return first, (tile + 1) * TILE

    @pl.when(step == 0)
    def _():
        acc[...] = jnp.zeros_like(acc)
        bounds = seg_bounds(blocks, pads, 0)
        v_ones[:, :HD] = kv[0, 1]
        v_ones[:, HD:] = jnp.ones((length, HD), BF16)
        for tile in range(length // TILE):
            first, last = window(tile)
            rows = tile * TILE + lax.broadcasted_iota(jnp.int32, (TILE, last - first), 0)
            cols = first + lax.broadcasted_iota(jnp.int32, (TILE, last - first), 1)
            starts = by_segment(rows, bounds, [b[0] for b in bounds])
            ends = by_segment(rows, bounds, [b[2] for b in bounds])
            seen = (cols >= starts) & (cols <= rows) & (cols < ends)
            bias[tile * TILE : (tile + 1) * TILE, : last - first] = jnp.where(seen, 0.0, -1e30)
            rows = tile * TILE + lax.broadcasted_iota(jnp.int32, (TILE, HD), 0)
            ends = by_segment(rows, bounds, [b[2] for b in bounds])
            live[tile * TILE : (tile + 1) * TILE, :] = jnp.where(rows < ends, 1.0, 0.0)

    for tile in range(length // TILE):
        first, last = window(tile)
        here = slice(tile * TILE, (tile + 1) * TILE)
        for pair in range(0, heads, 2):
            rows = jnp.concatenate(
                [q[0, here, h * HD : (h + 1) * HD] for h in (pair, pair + 1)], axis=0
            )
            scores = dot(rows, kv[0, 0, first:last, :], (1, 1)).reshape(2, TILE, last - first)
            scores = scores * factor + bias[here, : last - first][None]
            top = jnp.max(scores, axis=-1, keepdims=True)
            weights = jnp.exp2(scores - top).astype(BF16).reshape(2 * TILE, last - first)
            mixed = dot(weights, v_ones[first:last, :], (1, 0))
            for n, h in enumerate((pair, pair + 1)):
                part = mixed[n * TILE : (n + 1) * TILE]
                value = part[:, :HD] * (live[here, :] / part[:, HD:])
                att[here, h * HD : (h + 1) * HD] = value.astype(BF16)
    acc[...] += dot(att[...], down[0].reshape(slots * rank, -1), (1, 1))

    @pl.when(step == pl.num_programs(0) - 1)
    def _():
        bounds = seg_bounds(blocks, pads, 0)
        slot_row = by_segment(token_row(length), bounds, seg_slots(tenant, table, 0))
        out[...] = select_rows(acc[...].T, range(slots), slot_row, rank)


def grad_side_kernel(parts, blocks, pads, *refs):
    ranks, (grad, up, part_out, up_out, acc, spread) = refs[:parts], refs[parts:]
    step = pl.program_id(0)
    length = grad.shape[1]
    rank = part_out.shape[0]
    segs = up.shape[0] // rank
    bounds = seg_bounds(blocks, pads, 1)
    tokens = token_row(length)
    live = tokens < by_segment(tokens, bounds, [b[2] for b in bounds])
    seg_row = jnp.where(live, by_segment(tokens, bounds, list(range(segs))), -1)

    @pl.when(step == 0)
    def _():
        acc[...] = jnp.zeros_like(acc)
        total = sum(r[...] for r in ranks).astype(BF16).astype(F32)
        spread[...] = spread_rows(total, range(segs), seg_row).astype(BF16)

    block = grad[0]
    fill = jnp.zeros((acc.shape[1] - up.shape[0], up.shape[1]), BF16)
    acc[...] += dot(block, jnp.concatenate([up[...], fill], axis=0), (1, 1))
    up_out[...] = (SCALE * dot(spread[...], block, (1, 0))).astype(BF16)

    @pl.when(step == pl.num_programs(0) - 1)
    def _():
        part_out[...] = select_rows(acc[...].T, range(segs), seg_row, rank)


def grad_down_kernel(parts, blocks, pads, *refs):
    ranks, (saved, out, spread) = refs[:parts], refs[parts:]
    segs = blocks.shape[-1]

    @pl.when(pl.program_id(0) == 0)
    def _():
        bounds = seg_bounds(blocks, pads, 1)
        seg_row = by_segment(token_row(saved.shape[1]), bounds, list(range(segs)))
        total = (SCALE * sum(r[...] for r in ranks)).astype(BF16).astype(F32)
        spread[...] = spread_rows(total, range(segs), seg_row).astype(BF16)

    out[...] = dot(spread[...], saved[0], (1, 0)).astype(BF16)


def new_acts_kernel(parts, blocks, pads, tenant, table, *refs):
    ranks, (arrived, up, out, spread) = refs[:parts], refs[parts:]
    slots, rank = up.shape[1], up.shape[2]

    @pl.when(pl.program_id(0) == 0)
    def _():
        bounds = seg_bounds(blocks, pads, 0)
        slot_row = by_segment(token_row(arrived.shape[0]), bounds, seg_slots(tenant, table, 0))
        total = sum(r[...] for r in ranks).astype(BF16).astype(F32)
        spread[...] = spread_rows(total, range(slots), slot_row).T.astype(BF16)

    update = dot(spread[...], up[0].reshape(slots * rank, -1), (1, 0))
    out[0] = (arrived[...].astype(F32) + SCALE * update).astype(BF16)


def place_kernel(dp_axis, tenant, other_tenant, table, own_d, other_d, own_u, other_u, out_d, out_u):
    slots, rank = out_d.shape[1], out_d.shape[2]
    first = lax.axis_index(dp_axis) == 0
    own, other = seg_slots(tenant, table, 1), seg_slots(other_tenant, table, 1)
    keys = [jnp.where(first, a, b) for a, b in zip(own, other)]
    keys += [jnp.where(first, b, a) for a, b in zip(own, other)]
    for mine, peer, out in ((own_d, other_d, out_d), (own_u, other_u, out_u)):
        a, b = mine[...], peer[...]
        rows = jnp.concatenate([jnp.where(first, a, b), jnp.where(first, b, a)], axis=0)
        rows = rows.astype(F32)
        for slot in range(slots):
            total = jnp.zeros((rank, rows.shape[1]), F32)
            for i, key in enumerate(keys):
                total = total + jnp.where(key == slot, rows[i * rank : (i + 1) * rank], 0.0)
            out[0, slot] = total.astype(BF16)


def params(**more):
    return pltpu.CompilerParams(vmem_limit_bytes=VMEM_BYTES, **more)


def cost(flops, nbytes):
    return pl.CostEstimate(flops=flops, bytes_accessed=nbytes, transcendentals=0)


def whole(array):
    zeros = (0,) * array.ndim
    return pl.BlockSpec(array.shape, lambda *_: zeros)


def per_device(
    sizes,
    act_inbox,
    grad_inbox,
    queries,
    keys_values,
    saved_attn,
    down_adapt,
    up_adapt,
    seg_blocks,
    seg_pads,
    seg_tenant,
    adapter_table,
):
    n_section, n_tensor, n_dp = sizes["section"], sizes["tensor"], sizes["dp"]
    _, length, width = queries.shape
    _, slots, rank, _ = up_adapt.shape
    segs = seg_blocks.shape[-1]
    rows = slots * rank
    packed = segs * rank
    kv_heads = keys_values.shape[-1] // HD
    group = width // keys_values.shape[-1]
    meta = (seg_blocks, seg_pads, seg_tenant, adapter_table)
    half = pl.BlockSpec(memory_space=pltpu.VMEM)

    def section_shift(value, steps):
        pairs = [(i, (i + steps) % n_section) for i in range(n_section)]
        return lax.ppermute(value, "section", pairs)

    def dp_swap(value):
        return lax.ppermute(value, "dp", [(i, (i + 1) % n_dp) for i in range(n_dp)])

    def to_all_tensor(value, steps):
        got = []
        for k in range(n_tensor):
            if steps == 0 and k == 0:
                got.append(value)
                continue
            pairs = [
                (s * n_tensor + z, ((s + steps) % n_section) * n_tensor + (z + k) % n_tensor)
                for s in range(n_section)
                for z in range(n_tensor)
            ]
            got.append(lax.ppermute(value, ("section", "tensor"), pairs))
        return got

    arrived = section_shift(act_inbox[0], 1)

    up_packed = pl.pallas_call(
        pack_up_kernel,
        out_shape=jax.ShapeDtypeStruct((packed, width), BF16),
        in_specs=[SMEM, SMEM, half],
        out_specs=half,
        compiler_params=params(),
        cost_estimate=cost(0, 4 * packed * width),
        name="pack_up",
    )(seg_tenant, adapter_table, up_adapt)
    up_there = section_shift(up_packed, 1)
    blocks_there = section_shift(seg_blocks, 1)
    pads_there = section_shift(seg_pads, 1)

    cols = 1024
    steps = width // cols
    back_part = pl.pallas_call(
        saved_rank_kernel,
        grid=(steps,),
        out_shape=jax.ShapeDtypeStruct((rank, length), F32),
        in_specs=[SMEM] * 4
        + [
            pl.BlockSpec((1, length, cols), lambda i: (0, 0, i)),
            pl.BlockSpec((1, slots, rank, cols), lambda i: (0, 0, 0, i)),
        ],
        out_specs=pl.BlockSpec((rank, length), lambda i: (0, 0)),
        scratch_shapes=[pltpu.VMEM((length, rows), F32)],
        compiler_params=params(),
        cost_estimate=cost(2 * length * rows * width, 2 * length * width),
        name="saved_rank",
    )(*meta, saved_attn, down_adapt)
    back_parts = to_all_tensor(back_part, 1)

    heads = 4
    per_kv = group // heads

    def attend(kv_head):
        return pl.pallas_call(
            attend_kernel,
            grid=(per_kv,),
            out_shape=jax.ShapeDtypeStruct((rank, length), F32),
            in_specs=[SMEM] * 4
            + [
                pl.BlockSpec((1, length, heads * HD), lambda i: (0, 0, kv_head * per_kv + i)),
                pl.BlockSpec((1, 2, length, HD), lambda i: (0, 0, 0, kv_head)),
                pl.BlockSpec((1, slots, rank, heads * HD), lambda i: (0, 0, 0, kv_head * per_kv + i)),
            ],
            out_specs=pl.BlockSpec((rank, length), lambda i: (0, 0)),
            scratch_shapes=[
                pltpu.VMEM((length, rows), F32),
                pltpu.VMEM((length, MAX_SEG + TILE), F32),
                pltpu.VMEM((length, HD), F32),
                pltpu.VMEM((length, 2 * HD), BF16),
                pltpu.VMEM((length, heads * HD), BF16),
            ],
            compiler_params=params(),
            cost_estimate=cost(8 * length * length * group * HD, 2 * length * group * HD),
            name="attend",
        )(*meta, queries, keys_values, down_adapt)

    fwd_halves = [attend(0)]

    gated, back_parts, up_there = lax.optimization_barrier((grad_inbox, back_parts, up_there))
    grad_part, up_grad = pl.pallas_call(
        functools.partial(grad_side_kernel, n_tensor),
        grid=(steps,),
        out_shape=[
            jax.ShapeDtypeStruct((rank, length), F32),
            jax.ShapeDtypeStruct((packed, width), BF16),
        ],
        in_specs=[SMEM] * 2
        + [pl.BlockSpec((rank, length), lambda i: (0, 0))] * n_tensor
        + [
            pl.BlockSpec((1, length, cols), lambda i: (0, 0, i)),
            pl.BlockSpec((packed, cols), lambda i: (0, i)),
        ],
        out_specs=[
            pl.BlockSpec((rank, length), lambda i: (0, 0)),
            pl.BlockSpec((packed, cols), lambda i: (0, i)),
        ],
        scratch_shapes=[pltpu.VMEM((length, rows), F32), pltpu.VMEM((packed, length), BF16)],
        compiler_params=params(),
        cost_estimate=cost(4 * length * rows * width, 2 * length * width),
        name="grad_side",
    )(blocks_there, pads_there, *back_parts, gated, up_there)
    grad_parts = to_all_tensor(grad_part, -1)
    up_grad = section_shift(up_grad, -1)

    for kv_head in range(1, kv_heads):
        fwd_halves.append(attend(kv_head))
    fwd_parts = to_all_tensor(sum(fwd_halves), 0)

    down_grad = pl.pallas_call(
        functools.partial(grad_down_kernel, n_tensor),
        grid=(steps,),
        out_shape=jax.ShapeDtypeStruct((packed, width), BF16),
        in_specs=[SMEM] * 2
        + [pl.BlockSpec((rank, length), lambda i: (0, 0))] * n_tensor
        + [pl.BlockSpec((1, length, cols), lambda i: (0, 0, i))],
        out_specs=pl.BlockSpec((packed, cols), lambda i: (0, i)),
        scratch_shapes=[pltpu.VMEM((packed, length), BF16)],
        compiler_params=params(),
        cost_estimate=cost(2 * length * rows * width, 2 * length * width),
        name="grad_down",
    )(seg_blocks, seg_pads, *grad_parts, saved_attn)

    new_acts = pl.pallas_call(
        functools.partial(new_acts_kernel, n_tensor),
        grid=(steps,),
        out_shape=jax.ShapeDtypeStruct((1, length, width), BF16),
        in_specs=[SMEM] * 4
        + [pl.BlockSpec((rank, length), lambda i: (0, 0))] * n_tensor
        + [
            pl.BlockSpec((length, cols), lambda i: (0, i)),
            pl.BlockSpec((1, slots, rank, cols), lambda i: (0, 0, 0, i)),
        ],
        out_specs=pl.BlockSpec((1, length, cols), lambda i: (0, 0, i)),
        scratch_shapes=[pltpu.VMEM((length, rows), BF16)],
        compiler_params=params(),
        cost_estimate=cost(2 * length * rows * width, 4 * length * width),
        name="new_acts",
    )(*meta, *fwd_parts, arrived, up_adapt)

    if n_dp == 2:
        other_tenant = dp_swap(seg_tenant)
        other_up, other_down = dp_swap(up_grad), dp_swap(down_grad)
        block = pl.BlockSpec((packed, cols), lambda i: (0, i))
        out_block = pl.BlockSpec((1, slots, rank, cols), lambda i: (0, 0, 0, i))
        grad_down, grad_up = pl.pallas_call(
            functools.partial(place_kernel, "dp"),
            grid=(steps,),
            out_shape=[jax.ShapeDtypeStruct(up_adapt.shape, BF16)] * 2,
            in_specs=[SMEM] * 3 + [block] * 4,
            out_specs=[out_block] * 2,
            compiler_params=params(),
            cost_estimate=cost(0, 12 * rows * width),
            name="place",
        )(seg_tenant, other_tenant, adapter_table, down_grad, other_down, up_grad, other_up)
    else:
        seg_slot = adapter_table[seg_tenant[0, 1, 0]]
        onehot = (seg_slot[None, :] == jnp.arange(slots, dtype=jnp.int32)[:, None]).astype(F32)

        def placed(compact):
            full = jnp.einsum("as,srw->arw", onehot, compact.reshape(segs, rank, width).astype(F32))
            return lax.psum(full, "dp").astype(BF16)[None]

        grad_down, grad_up = placed(down_grad), placed(up_grad)
    return new_acts, grad_down, grad_up


def solution(mesh):
    wide = P("section", "dp", "tensor")
    adapter = P("section", None, None, "tensor")
    per_segment = P("section", None, "dp", None)
    return jax.shard_map(
        functools.partial(per_device, dict(mesh.shape)),
        mesh=mesh,
        in_specs=(
            wide,
            wide,
            wide,
            P("section", None, "dp", "tensor"),
            wide,
            adapter,
            adapter,
            per_segment,
            per_segment,
            per_segment,
            P(),
        ),
        out_specs=(wide, adapter, adapter),
        check_vma=False,
    )
```

```python
import functools
import math

import jax
import jax.numpy as jnp
from jax import lax
from jax.experimental import pallas as pl
from jax.experimental.pallas import tpu as pltpu
from jax.sharding import PartitionSpec as P

HD = 128
BLOCK = 64
MAX_SEG = 4 * BLOCK
TILE = 128
SCALE = 2.0
F32 = jnp.float32
BF16 = jnp.bfloat16
VMEM_BYTES = 60 * 1024 * 1024
CHUNK = 32
COLS = 1024
STEP_HEADS = 4

SMEM = pl.BlockSpec(memory_space=pltpu.SMEM)


def dot(left, right, dims):
    return lax.dot_general(left, right, ((dims[:1], dims[1:]), ((), ())), preferred_element_type=F32)


def seg_bounds(blocks, pads, batch):
    bounds, start = [], 0
    for i in range(blocks.shape[-1]):
        end = start + blocks[0, batch, 0, i] * BLOCK
        bounds.append((start, end, end - pads[0, batch, 0, i]))
        start = end
    return bounds


def seg_slots(tenant, table, batch):
    return [table[tenant[0, batch, 0, i]] for i in range(tenant.shape[-1])]


def by_segment(pos, bounds, values):
    out = jnp.zeros_like(pos) + values[0]
    for (start, _, _), value in zip(bounds[1:], values[1:]):
        out = jnp.where(pos >= start, value, out)
    return out


def select_rows(full, keys, key_row, rank):
    out = jnp.zeros((rank, full.shape[1]), F32)
    for i, key in enumerate(keys):
        out = out + jnp.where(key_row == key, full[i * rank : (i + 1) * rank], 0.0)
    return out


def spread_rows(ranked, keys, key_row):
    return jnp.concatenate([jnp.where(key_row == key, ranked, 0.0) for key in keys], axis=0)


def token_row(length):
    return lax.broadcasted_iota(jnp.int32, (1, length), 1)


class Kernel:
    def __init__(self, sizes, shapes):
        self.sections, self.tensors, self.dps = sizes["section"], sizes["tensor"], sizes["dp"]
        (_, self.length, self.width), self.kv_width, (_, self.slots, self.rank, _), self.segs = shapes
        self.rows = self.slots * self.rank
        self.packed = self.segs * self.rank
        self.kv_heads = self.kv_width // HD
        self.steps = self.width // (STEP_HEADS * HD)
        self.steps_per_kv = self.steps // self.kv_heads
        self.chunks = self.length // CHUNK

    def scratch(self):
        n, w, r, p = self.length, self.width, self.rank, self.packed
        dma = pltpu.SemaphoreType.DMA
        wide = pltpu.VMEM((n, w), BF16)
        adapter = pltpu.VMEM((self.slots, r, w), BF16)
        ranks = pltpu.VMEM((self.tensors, r, n), F32)
        one = pltpu.VMEM((r, n), F32)
        return dict(
            up_v=adapter,
            down_v=adapter,
            saved_v=wide,
            grad_v=wide,
            q_v=wide,
            kv_v=pltpu.VMEM((2, n, self.kv_width), BF16),
            up_send=pltpu.VMEM((p, w), BF16),
            up_in=pltpu.VMEM((p, w), BF16),
            tok=pltpu.VMEM((8, n), jnp.int32),
            tok_in=pltpu.VMEM((8, n), jnp.int32),
            tok_dp=pltpu.VMEM((self.dps, 8, n), jnp.int32),
            back_send=one,
            back_in=ranks,
            gp_send=one,
            gp_in=ranks,
            fwd_send=one,
            fwd_in=ranks,
            ug_send=pltpu.VMEM((p, w), BF16),
            ug_dp=pltpu.VMEM((self.dps, p, w), BF16),
            dg_dp=pltpu.VMEM((self.dps, p, w), BF16),
            arrived=wide,
            update=pltpu.VMEM((n, w), F32),
            acts_v=wide,
            gd_v=adapter,
            gu_v=adapter,
            acc=pltpu.VMEM((n, self.rows), F32),
            bias=pltpu.VMEM((n, MAX_SEG + TILE), F32),
            live=pltpu.VMEM((n, HD), F32),
            v_ones=pltpu.VMEM((self.kv_heads, n, 2 * HD), BF16),
            att=pltpu.VMEM((n, STEP_HEADS * HD), BF16),
            load_sem=dma((6,)),
            store_sem=dma((2,)),
            acts_sem=dma((self.chunks,)),
            up_sem=dma((2,)),
            tok_sem=dma((2,)),
            tok_dp_sem=dma((2, self.dps)),
            back_sem=dma((2, self.tensors)),
            gp_sem=dma((2, self.tensors)),
            fwd_sem=dma((2, self.tensors)),
            ug_sem=dma((2,)),
            ug_dp_sem=dma((2, self.dps)),
            dg_dp_sem=dma((2, self.dps)),
            act_sem=dma((2, self.chunks)),
        )

    def __call__(self, blocks, pads, tenant, table, act, grad, q, kv, saved, down, up, acts, gd, gu, **v):
        self.__dict__.update(v)
        self.meta = (blocks, pads, tenant, table)
        n, w, rank = self.length, self.width, self.rank
        me = {a: lax.axis_index(a) for a in ("section", "tensor", "dp")}

        def device(section=0, tensor=0, dp=0):
            return {
                "section": lax.rem(me["section"] + section + self.sections, self.sections),
                "tensor": lax.rem(me["tensor"] + tensor, self.tensors),
                "dp": lax.rem(me["dp"] + dp, self.dps),
            }

        def send(source, target, sems, where):
            return pltpu.make_async_remote_copy(
                src_ref=source,
                dst_ref=target,
                send_sem=sems[0],
                recv_sem=sems[1],
                device_id=where,
                device_id_type=pl.DeviceIdType.MESH,
            )

        def pair(sem, k):
            return sem.at[0, k], sem.at[1, k]

        def act_chunk(c):
            rows = pl.ds(pl.multiple_of(c * CHUNK, CHUNK), CHUNK)
            return send(
                act.at[0, rows, :], self.arrived.at[rows, :], pair(self.act_sem, c), device(section=1)
            )

        loads = [
            pltpu.make_async_copy(source, target, self.load_sem.at[i])
            for i, (source, target) in enumerate(
                (
                    (up.at[0], self.up_v),
                    (saved.at[0], self.saved_v),
                    (down.at[0], self.down_v),
                    (kv.at[0], self.kv_v),
                    (q.at[0], self.q_v),
                    (grad.at[0], self.grad_v),
                )
            )
        ]
        for load in loads:
            load.start()

        barrier = pltpu.get_barrier_semaphore()
        partners = [device(section=s, tensor=k) for s in (1, -1) for k in range(self.tensors)]
        partners += [device(tensor=k) for k in range(1, self.tensors)]
        partners += [device(dp=k) for k in range(1, self.dps)]
        for partner in partners:
            pl.semaphore_signal(
                barrier, inc=1, device_id=partner, device_id_type=pl.DeviceIdType.MESH
            )

        tokens = token_row(n)
        bounds = seg_bounds(blocks, pads, 1)
        slots = seg_slots(tenant, table, 1)
        alive = tokens < by_segment(tokens, bounds, [b[2] for b in bounds])
        line = lax.broadcasted_iota(jnp.int32, (8, n), 0)
        tok = jnp.where(alive, by_segment(tokens, bounds, list(range(self.segs))), -1) + 0 * line
        for i, slot in enumerate(slots):
            tok = jnp.where(line == i + 1, slot, tok)
        self.tok[...] = tok
        back_slot = by_segment(tokens, bounds, slots)

        loads[0].wait()
        for i, slot in enumerate(slots):
            self.up_send[i * rank : (i + 1) * rank, :] = self.up_v[slot]
        pl.semaphore_wait(barrier, len(partners))

        sent = []

        def start(copy):
            copy.start()
            sent.append(copy)
            return copy

        up_copy = start(send(self.up_send, self.up_in, (self.up_sem.at[0], self.up_sem.at[1]), device(section=1)))
        tok_copy = start(send(self.tok, self.tok_in, (self.tok_sem.at[0], self.tok_sem.at[1]), device(section=1)))
        act_chunk(0).start()
        tok_dp_copies = [
            start(send(self.tok, self.tok_dp.at[k], pair(self.tok_dp_sem, k), device(dp=k)))
            for k in range(1, self.dps)
        ]

        loads[1].wait()
        loads[2].wait()
        self.acc[...] = jnp.zeros_like(self.acc)

        @pl.loop(0, w // COLS)
        def _(i):
            cols = pl.ds(pl.multiple_of(i * COLS, COLS), COLS)
            right = self.down_v[:, :, cols].reshape(self.rows, COLS)
            self.acc[...] += dot(self.saved_v[:, cols], right, (1, 1))

        self.back_send[...] = select_rows(self.acc[...].T, range(self.slots), back_slot, rank)
        back_copies = [
            start(send(self.back_send, self.back_in.at[k], pair(self.back_sem, k), device(section=1, tensor=k)))
            for k in range(self.tensors)
        ]
        act_chunk(1).start()

        loads[3].wait()
        loads[4].wait()
        self.prepare_attention()
        self.acc[...] = jnp.zeros_like(self.acc)
        early, late = self.steps * 3 // 8, self.steps * 7 // 8

        def attend_steps(first, last):
            @pl.loop(first, last)
            def _(step):
                self.attend(step)
                act_chunk(2 + step).start()

        attend_steps(0, early)

        loads[5].wait()
        up_copy.wait_recv()
        tok_copy.wait_recv()
        for copy in back_copies:
            copy.wait_recv()
        seg_row = self.tok_in[0:1, :]
        total = sum(self.back_in[k] for k in range(self.tensors)).astype(BF16).astype(F32)
        spread = spread_rows(total, range(self.segs), seg_row).astype(BF16)
        fill = jnp.zeros((self.rows - self.packed, COLS), BF16)
        full = jnp.zeros((n, self.rows), F32)
        for i in range(w // COLS):
            cols = slice(i * COLS, (i + 1) * COLS)
            block = self.grad_v[:, cols]
            full = full + dot(block, jnp.concatenate([self.up_in[:, cols], fill], axis=0), (1, 1))
            self.ug_send[:, cols] = (SCALE * dot(spread, block, (1, 0))).astype(BF16)
        self.gp_send[...] = select_rows(full.T, range(self.segs), seg_row, rank)
        gp_copies = [
            start(send(self.gp_send, self.gp_in.at[k], pair(self.gp_sem, k), device(section=-1, tensor=k)))
            for k in range(self.tensors)
        ]
        ug_copy = start(send(self.ug_send, self.ug_dp.at[0], (self.ug_sem.at[0], self.ug_sem.at[1]), device(section=-1)))

        attend_steps(early, late)

        ug_copy.wait_recv()
        ug_dp_copies = [
            start(send(self.ug_dp.at[0], self.ug_dp.at[k], pair(self.ug_dp_sem, k), device(dp=k)))
            for k in range(1, self.dps)
        ]
        for copy in gp_copies:
            copy.wait_recv()
        total = SCALE * sum(self.gp_in[k] for k in range(self.tensors))
        spread = spread_rows(total.astype(BF16).astype(F32), range(self.segs), self.tok[0:1, :]).astype(BF16)
        for i in range(w // COLS):
            cols = slice(i * COLS, (i + 1) * COLS)
            self.dg_dp[0, :, cols] = dot(spread, self.saved_v[:, cols], (1, 0)).astype(BF16)
        dg_dp_copies = [
            start(send(self.dg_dp.at[0], self.dg_dp.at[k], pair(self.dg_dp_sem, k), device(dp=k)))
            for k in range(1, self.dps)
        ]

        attend_steps(late, self.steps)

        bounds = seg_bounds(blocks, pads, 0)
        fwd_slot = by_segment(tokens, bounds, seg_slots(tenant, table, 0))
        fwd_part = select_rows(self.acc[...].T, range(self.slots), fwd_slot, rank)
        self.fwd_send[...] = fwd_part
        fwd_copies = [
            start(send(self.fwd_send, self.fwd_in.at[k], pair(self.fwd_sem, k), device(tensor=k)))
            for k in range(1, self.tensors)
        ]
        for copy in fwd_copies:
            copy.wait_recv()
        total = fwd_part + sum(self.fwd_in[k] for k in range(1, self.tensors))
        total = total.astype(BF16).astype(F32)
        spread = spread_rows(total, range(self.slots), fwd_slot).T.astype(BF16)
        for i in range(w // COLS):
            cols = slice(i * COLS, (i + 1) * COLS)
            right = self.up_v[:, :, cols].reshape(self.rows, COLS)
            self.update[:, cols] = SCALE * dot(spread, right, (1, 0))

        issued = 2 + self.steps

        def acts_out(c):
            rows = pl.ds(pl.multiple_of(c * CHUNK, CHUNK), CHUNK)
            return pltpu.make_async_copy(self.acts_v.at[rows, :], acts.at[0, rows, :], self.acts_sem.at[c])

        def add_chunks(first, last):
            @pl.loop(first, last)
            def _(c):
                @pl.when(c + issued < self.chunks)
                def _():
                    act_chunk(c + issued).start()

                act_chunk(c).wait_recv()
                rows = pl.ds(pl.multiple_of(c * CHUNK, CHUNK), CHUNK)
                added = self.arrived[rows, :].astype(F32) + self.update[rows, :]
                self.acts_v[rows, :] = added.astype(BF16)
                acts_out(c).start()

        before = self.chunks * 3 // 4
        add_chunks(0, before)
        for copy in tok_dp_copies + ug_dp_copies + dg_dp_copies:
            copy.wait_recv()
        self.tok_dp[0] = self.tok[...]
        self.place(self.dg_dp, self.gd_v, me["dp"])
        self.place(self.ug_dp, self.gu_v, me["dp"])
        stores = [
            pltpu.make_async_copy(self.gd_v, gd.at[0], self.store_sem.at[0]),
            pltpu.make_async_copy(self.gu_v, gu.at[0], self.store_sem.at[1]),
        ]
        for store in stores:
            store.start()
        add_chunks(before, self.chunks)

        for store in stores:
            store.wait()
        for copy in sent:
            copy.wait_send()

        @pl.loop(0, self.chunks)
        def _(c):
            act_chunk(c).wait_send()
            acts_out(c).wait()

    def window(self, tile):
        return max(0, tile * TILE - MAX_SEG), (tile + 1) * TILE

    def prepare_attention(self):
        blocks, pads = self.meta[:2]
        bounds = seg_bounds(blocks, pads, 0)
        for head in range(self.kv_heads):
            self.v_ones[head, :, :HD] = self.kv_v[1, :, head * HD : (head + 1) * HD]
            self.v_ones[head, :, HD:] = jnp.ones((self.length, HD), BF16)
        for tile in range(self.length // TILE):
            first, last = self.window(tile)
            here = slice(tile * TILE, (tile + 1) * TILE)
            rows = tile * TILE + lax.broadcasted_iota(jnp.int32, (TILE, last - first), 0)
            cols = first + lax.broadcasted_iota(jnp.int32, (TILE, last - first), 1)
            starts = by_segment(rows, bounds, [b[0] for b in bounds])
            ends = by_segment(rows, bounds, [b[2] for b in bounds])
            seen = (cols >= starts) & (cols <= rows) & (cols < ends)
            self.bias[here, : last - first] = jnp.where(seen, 0.0, -1e30)
            rows = tile * TILE + lax.broadcasted_iota(jnp.int32, (TILE, HD), 0)
            ends = by_segment(rows, bounds, [b[2] for b in bounds])
            self.live[here, :] = jnp.where(rows < ends, 1.0, 0.0)

    def attend(self, step):
        factor = math.log2(math.e) / math.sqrt(HD)
        span = STEP_HEADS * HD
        base = pl.multiple_of(step * span, span)
        head = step // self.steps_per_kv
        key_cols = pl.ds(pl.multiple_of(head * HD, HD), HD)
        for tile in range(self.length // TILE):
            first, last = self.window(tile)
            here = slice(tile * TILE, (tile + 1) * TILE)
            block = self.q_v[here, pl.ds(base, span)]
            for two in range(0, STEP_HEADS, 2):
                queries = jnp.concatenate(
                    [block[:, h * HD : (h + 1) * HD] for h in (two, two + 1)], axis=0
                )
                scores = dot(queries, self.kv_v[0, first:last, key_cols], (1, 1))
                scores = scores.reshape(2, TILE, last - first)
                scores = scores * factor + self.bias[here, : last - first][None]
                top = jnp.max(scores, axis=-1, keepdims=True)
                weights = jnp.exp2(scores - top).astype(BF16).reshape(2 * TILE, last - first)
                mixed = dot(weights, self.v_ones[head, first:last, :], (1, 0))
                for i, h in enumerate((two, two + 1)):
                    part = mixed[i * TILE : (i + 1) * TILE]
                    value = part[:, :HD] * (self.live[here, :] / part[:, HD:])
                    self.att[here, h * HD : (h + 1) * HD] = value.astype(BF16)
        right = self.down_v[:, :, pl.ds(base, span)].reshape(self.rows, span)
        self.acc[...] += dot(self.att[...], right, (1, 1))

    def place(self, compact, out, my_dp):
        rank, n = self.rank, self.length

        @pl.loop(0, self.width // n)
        def _(i):
            cols = pl.ds(pl.multiple_of(i * n, n), n)
            totals = [jnp.zeros((rank, n), F32)] * self.slots
            for d in range(self.dps):
                k = lax.rem(my_dp - d + self.dps, self.dps)
                for s in range(self.segs):
                    key = self.tok_dp[k, s + 1 : s + 2, :]
                    rows = compact[k, s * rank : (s + 1) * rank, cols].astype(F32)
                    for slot in range(self.slots):
                        totals[slot] = totals[slot] + jnp.where(key == slot, rows, 0.0)
            for slot in range(self.slots):
                out[slot, :, cols] = totals[slot].astype(BF16)


def per_device(sizes, act, grad, queries, keys_values, saved, down, up, blocks, pads, tenant, table):
    kernel = Kernel(sizes, (queries.shape, keys_values.shape[-1], up.shape, blocks.shape[-1]))
    scratch = kernel.scratch()
    names = list(scratch)

    def body(*refs):
        kernel(*refs[: -len(names)], **dict(zip(names, refs[-len(names) :])))

    return tuple(
        pl.pallas_call(
            body,
            out_shape=[jax.ShapeDtypeStruct(a.shape, BF16) for a in (act, down, up)],
            in_specs=[SMEM] * 4 + [pl.BlockSpec(memory_space=pl.ANY)] * 7,
            out_specs=[pl.BlockSpec(memory_space=pl.ANY)] * 3,
            scratch_shapes=list(scratch.values()),
            compiler_params=pltpu.CompilerParams(
                vmem_limit_bytes=VMEM_BYTES, collective_id=0, has_side_effects=True
            ),
            name="adapter_step",
        )(blocks, pads, tenant, table, act, grad, queries, keys_values, saved, down, up)
    )


def solution(mesh):
    wide = P("section", "dp", "tensor")
    adapter = P("section", None, None, "tensor")
    per_segment = P("section", None, "dp", None)
    return jax.shard_map(
        functools.partial(per_device, dict(mesh.shape)),
        mesh=mesh,
        in_specs=(
            wide,
            wide,
            wide,
            P("section", None, "dp", "tensor"),
            wide,
            adapter,
            adapter,
            per_segment,
            per_segment,
            per_segment,
            P(),
        ),
        out_specs=(wide, adapter, adapter),
        check_vma=False,
    )
```

```python
import functools
import math

import jax
import jax.numpy as jnp
from jax import lax
from jax.experimental import pallas as pl
from jax.experimental.pallas import tpu as pltpu
from jax.sharding import PartitionSpec as P

HD = 128
BLOCK = 64
MAX_SEG = 4 * BLOCK
TILE = 128
SCALE = 2.0
F32 = jnp.float32
BF16 = jnp.bfloat16
VMEM_BYTES = 50 * 1024 * 1024
CHUNK = 32
COLS = 1024
STEP_HEADS = 4

SMEM = pl.BlockSpec(memory_space=pltpu.SMEM)


def dot(left, right, dims):
    return lax.dot_general(left, right, ((dims[:1], dims[1:]), ((), ())), preferred_element_type=F32)


def seg_bounds(blocks, pads, batch):
    bounds, start = [], 0
    for i in range(blocks.shape[-1]):
        end = start + blocks[0, batch, 0, i] * BLOCK
        bounds.append((start, end, end - pads[0, batch, 0, i]))
        start = end
    return bounds


def seg_slots(tenant, table, batch):
    return [table[tenant[0, batch, 0, i]] for i in range(tenant.shape[-1])]


def by_segment(pos, bounds, values):
    out = jnp.zeros_like(pos) + values[0]
    for (start, _, _), value in zip(bounds[1:], values[1:]):
        out = jnp.where(pos >= start, value, out)
    return out


def select_rows(full, keys, key_row, rank):
    out = jnp.zeros((rank, full.shape[1]), F32)
    for i, key in enumerate(keys):
        out = out + jnp.where(key_row == key, full[i * rank : (i + 1) * rank], 0.0)
    return out


def spread_rows(ranked, keys, key_row):
    return jnp.concatenate([jnp.where(key_row == key, ranked, 0.0) for key in keys], axis=0)


def token_row(length):
    return lax.broadcasted_iota(jnp.int32, (1, length), 1)


class Kernel:
    def __init__(self, sizes, shapes):
        self.sections, self.tensors, self.dps = sizes["section"], sizes["tensor"], sizes["dp"]
        (_, self.length, self.width), self.kv_width, (_, self.slots, self.rank, _), self.segs = shapes
        self.rows = self.slots * self.rank
        self.packed = self.segs * self.rank
        self.kv_heads = self.kv_width // HD
        self.steps = self.width // (STEP_HEADS * HD)
        self.steps_per_kv = self.steps // self.kv_heads
        self.chunks = self.length // CHUNK

    def scratch(self):
        n, w, r, p = self.length, self.width, self.rank, self.packed
        dma = pltpu.SemaphoreType.DMA
        wide = pltpu.VMEM((n, w), BF16)
        adapter = pltpu.VMEM((self.slots, r, w), BF16)
        ranks = pltpu.VMEM((self.tensors, r, n), F32)
        one = pltpu.VMEM((r, n), F32)
        half = pltpu.VMEM((r, n), BF16)
        return dict(
            up_v=adapter,
            down_v=adapter,
            saved_v=wide,
            grad_v=wide,
            q_v=wide,
            kv_v=pltpu.VMEM((2, n, self.kv_width), BF16),
            up_send=pltpu.VMEM((p, w), BF16),
            up_in=pltpu.VMEM((p, w), BF16),
            tok=pltpu.VMEM((8, n), jnp.int32),
            tok_in=pltpu.VMEM((8, n), jnp.int32),
            tok_dp=pltpu.VMEM((self.dps, 8, n), jnp.int32),
            back_send=one,
            back_in=ranks,
            back_sum=half,
            back_there=half,
            gp_send=one,
            gp_in=ranks,
            gp_sum=half,
            gp_there=half,
            fwd_send=one,
            fwd_in=ranks,
            ug_send=pltpu.VMEM((p, w), BF16),
            ug_dp=pltpu.VMEM((self.dps, p, w), BF16),
            dg_dp=pltpu.VMEM((self.dps, p, w), BF16),
            arrived=wide,
            update=pltpu.VMEM((n, w), F32),
            acc=pltpu.VMEM((n, self.rows), F32),
            bias=pltpu.VMEM((n, MAX_SEG + TILE), F32),
            live=pltpu.VMEM((n, HD), F32),
            v_ones=pltpu.VMEM((self.kv_heads, n, 2 * HD), BF16),
            att=pltpu.VMEM((n, STEP_HEADS * HD), BF16),
            load_sem=dma((6,)),
            up_sem=dma((2,)),
            tok_sem=dma((2,)),
            tok_dp_sem=dma((2, self.dps)),
            back_sem=dma((2, self.tensors)),
            gp_sem=dma((2, self.tensors)),
            fwd_sem=dma((2, self.tensors)),
            back_sum_sem=dma((2,)),
            gp_sum_sem=dma((2,)),
            ug_sem=dma((2,)),
            ug_dp_sem=dma((2, self.dps)),
            dg_dp_sem=dma((2, self.dps)),
            act_sem=dma((2, self.chunks)),
        )

    def __call__(self, blocks, pads, tenant, table, act, grad, q, kv, saved, down, up, acts, gd, gu, **v):
        self.__dict__.update(v)
        self.meta = (blocks, pads, tenant, table)
        n, w, rank = self.length, self.width, self.rank
        me = {a: lax.axis_index(a) for a in ("section", "tensor", "dp")}

        def device(section=0, tensor=0, dp=0):
            return {
                "section": lax.rem(me["section"] + section + self.sections, self.sections),
                "tensor": lax.rem(me["tensor"] + tensor, self.tensors),
                "dp": lax.rem(me["dp"] + dp, self.dps),
            }

        def send(source, target, sems, where):
            return pltpu.make_async_remote_copy(
                src_ref=source,
                dst_ref=target,
                send_sem=sems[0],
                recv_sem=sems[1],
                device_id=where,
                device_id_type=pl.DeviceIdType.MESH,
            )

        def pair(sem, k):
            return sem.at[0, k], sem.at[1, k]

        def act_chunk(c):
            rows = pl.ds(pl.multiple_of(c * CHUNK, CHUNK), CHUNK)
            return send(
                act.at[0, rows, :], self.arrived.at[rows, :], pair(self.act_sem, c), device(section=1)
            )

        loads = [
            pltpu.make_async_copy(source, target, self.load_sem.at[i])
            for i, (source, target) in enumerate(
                (
                    (up.at[0], self.up_v),
                    (saved.at[0], self.saved_v),
                    (down.at[0], self.down_v),
                    (kv.at[0], self.kv_v),
                    (q.at[0], self.q_v),
                    (grad.at[0], self.grad_v),
                )
            )
        ]
        for load in loads:
            load.start()

        barrier = pltpu.get_barrier_semaphore()
        partners = [device(section=s) for s in (1, -1)]
        partners += [device(tensor=k) for k in range(1, self.tensors)]
        partners += [device(dp=k) for k in range(1, self.dps)]
        for partner in partners:
            pl.semaphore_signal(
                barrier, inc=1, device_id=partner, device_id_type=pl.DeviceIdType.MESH
            )

        tokens = token_row(n)
        bounds = seg_bounds(blocks, pads, 1)
        slots = seg_slots(tenant, table, 1)
        alive = tokens < by_segment(tokens, bounds, [b[2] for b in bounds])
        line = lax.broadcasted_iota(jnp.int32, (8, n), 0)
        tok = jnp.where(alive, by_segment(tokens, bounds, list(range(self.segs))), -1) + 0 * line
        for i, slot in enumerate(slots):
            tok = jnp.where(line == i + 1, slot, tok)
        self.tok[...] = tok
        back_slot = by_segment(tokens, bounds, slots)

        loads[0].wait()
        for i, slot in enumerate(slots):
            self.up_send[i * rank : (i + 1) * rank, :] = self.up_v[slot]
        pl.semaphore_wait(barrier, len(partners))

        sent = []

        def start(copy):
            copy.start()
            sent.append(copy)
            return copy

        def to_tensor(part, source, target, sem):
            source[...] = part
            return [
                start(send(source, target.at[k], pair(sem, k), device(tensor=k)))
                for k in range(1, self.tensors)
            ]

        def tensor_sum(copies, source, target):
            for copy in copies:
                copy.wait_recv()
            return source[...] + sum(target[k] for k in range(1, self.tensors))

        up_copy = start(send(self.up_send, self.up_in, (self.up_sem.at[0], self.up_sem.at[1]), device(section=1)))
        tok_copy = start(send(self.tok, self.tok_in, (self.tok_sem.at[0], self.tok_sem.at[1]), device(section=1)))
        act_chunk(0).start()
        tok_dp_copies = [
            start(send(self.tok, self.tok_dp.at[k], pair(self.tok_dp_sem, k), device(dp=k)))
            for k in range(1, self.dps)
        ]

        loads[1].wait()
        loads[2].wait()
        self.acc[...] = jnp.zeros_like(self.acc)

        @pl.loop(0, w // COLS)
        def _(i):
            cols = pl.ds(pl.multiple_of(i * COLS, COLS), COLS)
            right = self.down_v[:, :, cols].reshape(self.rows, COLS)
            self.acc[...] += dot(self.saved_v[:, cols], right, (1, 1))

        back_part = select_rows(self.acc[...].T, range(self.slots), back_slot, rank)
        back_copies = to_tensor(back_part, self.back_send, self.back_in, self.back_sem)
        act_chunk(1).start()

        loads[3].wait()
        loads[4].wait()
        self.prepare_attention()
        self.acc[...] = jnp.zeros_like(self.acc)
        few = max(1, self.steps // 8)
        early, late = self.steps * 3 // 8, self.steps * 7 // 8

        def attend_steps(first, last):
            @pl.loop(first, last)
            def _(step):
                self.attend(step)
                act_chunk(2 + step).start()

        attend_steps(0, few)
        self.back_sum[...] = tensor_sum(back_copies, self.back_send, self.back_in).astype(BF16)
        back_copy = start(
            send(self.back_sum, self.back_there, (self.back_sum_sem.at[0], self.back_sum_sem.at[1]), device(section=1))
        )
        attend_steps(few, early)

        loads[5].wait()
        up_copy.wait_recv()
        tok_copy.wait_recv()
        back_copy.wait_recv()
        seg_row = self.tok_in[0:1, :]
        total = self.back_there[...].astype(F32)
        spread = spread_rows(total, range(self.segs), seg_row).astype(BF16)
        fill = jnp.zeros((self.rows - self.packed, COLS), BF16)
        full = jnp.zeros((n, self.rows), F32)
        for i in range(w // COLS):
            cols = slice(i * COLS, (i + 1) * COLS)
            block = self.grad_v[:, cols]
            full = full + dot(block, jnp.concatenate([self.up_in[:, cols], fill], axis=0), (1, 1))
            self.ug_send[:, cols] = (SCALE * dot(spread, block, (1, 0))).astype(BF16)
        gp_part = select_rows(full.T, range(self.segs), seg_row, rank)
        gp_copies = to_tensor(gp_part, self.gp_send, self.gp_in, self.gp_sem)
        ug_copy = start(send(self.ug_send, self.ug_dp.at[0], (self.ug_sem.at[0], self.ug_sem.at[1]), device(section=-1)))

        attend_steps(early, early + few)
        total = tensor_sum(gp_copies, self.gp_send, self.gp_in)
        self.gp_sum[...] = (SCALE * total).astype(BF16)
        gp_copy = start(
            send(self.gp_sum, self.gp_there, (self.gp_sum_sem.at[0], self.gp_sum_sem.at[1]), device(section=-1))
        )
        attend_steps(early + few, late)

        ug_copy.wait_recv()
        ug_dp_copies = [
            start(send(self.ug_dp.at[0], self.ug_dp.at[k], pair(self.ug_dp_sem, k), device(dp=k)))
            for k in range(1, self.dps)
        ]
        gp_copy.wait_recv()
        total = self.gp_there[...].astype(F32)
        spread = spread_rows(total, range(self.segs), self.tok[0:1, :]).astype(BF16)
        for i in range(w // COLS):
            cols = slice(i * COLS, (i + 1) * COLS)
            self.dg_dp[0, :, cols] = dot(spread, self.saved_v[:, cols], (1, 0)).astype(BF16)
        dg_dp_copies = [
            start(send(self.dg_dp.at[0], self.dg_dp.at[k], pair(self.dg_dp_sem, k), device(dp=k)))
            for k in range(1, self.dps)
        ]

        attend_steps(late, self.steps)

        bounds = seg_bounds(blocks, pads, 0)
        fwd_slot = by_segment(tokens, bounds, seg_slots(tenant, table, 0))
        fwd_part = select_rows(self.acc[...].T, range(self.slots), fwd_slot, rank)
        fwd_copies = to_tensor(fwd_part, self.fwd_send, self.fwd_in, self.fwd_sem)
        total = tensor_sum(fwd_copies, self.fwd_send, self.fwd_in).astype(BF16).astype(F32)
        spread = spread_rows(total, range(self.slots), fwd_slot).T.astype(BF16)
        for i in range(w // COLS):
            cols = slice(i * COLS, (i + 1) * COLS)
            right = self.up_v[:, :, cols].reshape(self.rows, COLS)
            self.update[:, cols] = SCALE * dot(spread, right, (1, 0))

        issued = 2 + self.steps

        def add_chunks(first, last):
            @pl.loop(first, last)
            def _(c):
                @pl.when(c + issued < self.chunks)
                def _():
                    act_chunk(c + issued).start()

                act_chunk(c).wait_recv()
                rows = pl.ds(pl.multiple_of(c * CHUNK, CHUNK), CHUNK)
                added = self.arrived[rows, :].astype(F32) + self.update[rows, :]
                acts[0, rows, :] = added.astype(BF16)

        before = self.chunks * 3 // 4
        add_chunks(0, before)
        for copy in tok_dp_copies + ug_dp_copies + dg_dp_copies:
            copy.wait_recv()
        self.tok_dp[0] = self.tok[...]
        self.place(self.dg_dp, gd, me["dp"])
        self.place(self.ug_dp, gu, me["dp"])
        add_chunks(before, self.chunks)

        for copy in sent:
            copy.wait_send()

        @pl.loop(0, self.chunks)
        def _(c):
            act_chunk(c).wait_send()

    def window(self, tile):
        return max(0, tile * TILE - MAX_SEG), (tile + 1) * TILE

    def prepare_attention(self):
        blocks, pads = self.meta[:2]
        bounds = seg_bounds(blocks, pads, 0)
        for head in range(self.kv_heads):
            self.v_ones[head, :, :HD] = self.kv_v[1, :, head * HD : (head + 1) * HD]
            self.v_ones[head, :, HD:] = jnp.ones((self.length, HD), BF16)
        for tile in range(self.length // TILE):
            first, last = self.window(tile)
            here = slice(tile * TILE, (tile + 1) * TILE)
            rows = tile * TILE + lax.broadcasted_iota(jnp.int32, (TILE, last - first), 0)
            cols = first + lax.broadcasted_iota(jnp.int32, (TILE, last - first), 1)
            starts = by_segment(rows, bounds, [b[0] for b in bounds])
            ends = by_segment(rows, bounds, [b[2] for b in bounds])
            seen = (cols >= starts) & (cols <= rows) & (cols < ends)
            self.bias[here, : last - first] = jnp.where(seen, 0.0, -1e30)
            rows = tile * TILE + lax.broadcasted_iota(jnp.int32, (TILE, HD), 0)
            ends = by_segment(rows, bounds, [b[2] for b in bounds])
            self.live[here, :] = jnp.where(rows < ends, 1.0, 0.0)

    def attend(self, step):
        factor = math.log2(math.e) / math.sqrt(HD)
        span = STEP_HEADS * HD
        base = pl.multiple_of(step * span, span)
        head = step // self.steps_per_kv
        key_cols = pl.ds(pl.multiple_of(head * HD, HD), HD)
        for tile in range(self.length // TILE):
            first, last = self.window(tile)
            here = slice(tile * TILE, (tile + 1) * TILE)
            block = self.q_v[here, pl.ds(base, span)]
            for two in range(0, STEP_HEADS, 2):
                queries = jnp.concatenate(
                    [block[:, h * HD : (h + 1) * HD] for h in (two, two + 1)], axis=0
                )
                scores = dot(queries, self.kv_v[0, first:last, key_cols], (1, 1))
                scores = scores.reshape(2, TILE, last - first)
                scores = scores * factor + self.bias[here, : last - first][None]
                top = jnp.max(scores, axis=-1, keepdims=True)
                weights = jnp.exp2(scores - top).astype(BF16).reshape(2 * TILE, last - first)
                mixed = dot(weights, self.v_ones[head, first:last, :], (1, 0))
                for i, h in enumerate((two, two + 1)):
                    part = mixed[i * TILE : (i + 1) * TILE]
                    value = part[:, :HD] * (self.live[here, :] / part[:, HD:])
                    self.att[here, h * HD : (h + 1) * HD] = value.astype(BF16)
        right = self.down_v[:, :, pl.ds(base, span)].reshape(self.rows, span)
        self.acc[...] += dot(self.att[...], right, (1, 1))

    def place(self, compact, out, my_dp):
        rank, n = self.rank, self.length

        @pl.loop(0, self.width // n)
        def _(i):
            cols = pl.ds(pl.multiple_of(i * n, n), n)
            totals = [jnp.zeros((rank, n), F32)] * self.slots
            for d in range(self.dps):
                k = lax.rem(my_dp - d + self.dps, self.dps)
                for s in range(self.segs):
                    key = self.tok_dp[k, s + 1 : s + 2, :]
                    rows = compact[k, s * rank : (s + 1) * rank, cols].astype(F32)
                    for slot in range(self.slots):
                        totals[slot] = totals[slot] + jnp.where(key == slot, rows, 0.0)
            for slot in range(self.slots):
                out[0, slot, :, cols] = totals[slot].astype(BF16)


def per_device(sizes, act, grad, queries, keys_values, saved, down, up, blocks, pads, tenant, table):
    kernel = Kernel(sizes, (queries.shape, keys_values.shape[-1], up.shape, blocks.shape[-1]))
    scratch = kernel.scratch()
    names = list(scratch)

    def body(*refs):
        kernel(*refs[: -len(names)], **dict(zip(names, refs[-len(names) :])))

    return tuple(
        pl.pallas_call(
            body,
            out_shape=[pltpu.VMEM(a.shape, BF16) for a in (act, down, up)],
            in_specs=[SMEM] * 4 + [pl.BlockSpec(memory_space=pl.ANY)] * 7,
            out_specs=[pl.BlockSpec(memory_space=pltpu.VMEM)] * 3,
            scratch_shapes=list(scratch.values()),
            compiler_params=pltpu.CompilerParams(
                vmem_limit_bytes=VMEM_BYTES, collective_id=0, has_side_effects=True
            ),
            name="adapter_step",
        )(
            blocks,
            pads,
            tenant,
            table,
            *[
                pltpu.with_memory_space_constraint(a, pltpu.HBM)
                for a in (act, grad, queries, keys_values, saved, down, up)
            ],
        )
    )


def solution(mesh):
    wide = P("section", "dp", "tensor")
    adapter = P("section", None, None, "tensor")
    per_segment = P("section", None, "dp", None)
    return jax.shard_map(
        functools.partial(per_device, dict(mesh.shape)),
        mesh=mesh,
        in_specs=(
            wide,
            wide,
            wide,
            P("section", None, "dp", "tensor"),
            wide,
            adapter,
            adapter,
            per_segment,
            per_segment,
            per_segment,
            P(),
        ),
        out_specs=(wide, adapter, adapter),
        check_vma=False,
    )
```

```python
import functools
import math

import jax
import jax.numpy as jnp
from jax import lax
from jax.experimental import pallas as pl
from jax.experimental.pallas import tpu as pltpu
from jax.sharding import PartitionSpec as P

HD = 128
BLOCK = 64
MAX_SEG = 4 * BLOCK
TILE = 128
SCALE = 2.0
F32 = jnp.float32
BF16 = jnp.bfloat16
VMEM_BYTES = 50 * 1024 * 1024
CHUNK = 32
COLS = 1024
STEP_HEADS = 4
WRITES = 4

SMEM = pl.BlockSpec(memory_space=pltpu.SMEM)


def dot(left, right, dims):
    return lax.dot_general(left, right, ((dims[:1], dims[1:]), ((), ())), preferred_element_type=F32)


def seg_bounds(blocks, pads, batch):
    bounds, start = [], 0
    for i in range(blocks.shape[-1]):
        end = start + blocks[0, batch, 0, i] * BLOCK
        bounds.append((start, end, end - pads[0, batch, 0, i]))
        start = end
    return bounds


def seg_slots(tenant, table, batch):
    return [table[tenant[0, batch, 0, i]] for i in range(tenant.shape[-1])]


def by_segment(pos, bounds, values):
    out = jnp.zeros_like(pos) + values[0]
    for (start, _, _), value in zip(bounds[1:], values[1:]):
        out = jnp.where(pos >= start, value, out)
    return out


def select_rows(full, keys, key_row, rank):
    out = jnp.zeros((rank, full.shape[1]), F32)
    for i, key in enumerate(keys):
        out = out + jnp.where(key_row == key, full[i * rank : (i + 1) * rank], 0.0)
    return out


def spread_rows(ranked, keys, key_row):
    return jnp.concatenate([jnp.where(key_row == key, ranked, 0.0) for key in keys], axis=0)


def token_row(length):
    return lax.broadcasted_iota(jnp.int32, (1, length), 1)


class Kernel:
    def __init__(self, sizes, shapes):
        self.sections, self.tensors, self.dps = sizes["section"], sizes["tensor"], sizes["dp"]
        (_, self.length, self.width), self.kv_width, (_, self.slots, self.rank, _), self.segs = shapes
        self.rows = self.slots * self.rank
        self.packed = self.segs * self.rank
        self.kv_heads = self.kv_width // HD
        self.steps = self.width // (STEP_HEADS * HD)
        self.steps_per_kv = self.steps // self.kv_heads
        self.chunks = self.length // CHUNK

    def scratch(self):
        n, w, r, p = self.length, self.width, self.rank, self.packed
        dma = pltpu.SemaphoreType.DMA
        wide = pltpu.VMEM((n, w), BF16)
        adapter = pltpu.VMEM((self.slots, r, w), BF16)
        ranks = pltpu.VMEM((self.tensors, r, n), F32)
        one = pltpu.VMEM((r, n), F32)
        half = pltpu.VMEM((r, n), BF16)
        return dict(
            up_v=adapter,
            down_v=adapter,
            saved_v=wide,
            grad_v=wide,
            q_v=wide,
            kv_v=pltpu.VMEM((2, n, self.kv_width), BF16),
            up_send=pltpu.VMEM((p, w), BF16),
            up_in=pltpu.VMEM((p, w), BF16),
            tok=pltpu.VMEM((8, n), jnp.int32),
            tok_in=pltpu.VMEM((8, n), jnp.int32),
            tok_dp=pltpu.VMEM((self.dps, 8, n), jnp.int32),
            back_send=one,
            back_in=ranks,
            back_sum=half,
            back_there=half,
            gp_send=one,
            gp_in=ranks,
            gp_sum=half,
            gp_there=half,
            fwd_send=one,
            fwd_in=ranks,
            ug_send=pltpu.VMEM((p, w), BF16),
            ug_dp=pltpu.VMEM((self.dps, p, w), BF16),
            dg_dp=pltpu.VMEM((self.dps, p, w), BF16),
            arrived=wide,
            update=pltpu.VMEM((n, w), F32),
            acts_v=wide,
            gd_v=adapter,
            gu_v=adapter,
            acc=pltpu.VMEM((n, self.rows), F32),
            bias=pltpu.VMEM((n, MAX_SEG + TILE), F32),
            live=pltpu.VMEM((n, HD), F32),
            v_ones=pltpu.VMEM((self.kv_heads, n, 2 * HD), BF16),
            att=pltpu.VMEM((n, STEP_HEADS * HD), BF16),
            load_sem=dma((6,)),
            store_sem=dma((2,)),
            acts_sem=dma((self.chunks,)),
            up_sem=dma((2,)),
            tok_sem=dma((2,)),
            tok_dp_sem=dma((2, self.dps)),
            back_sem=dma((2, self.tensors)),
            gp_sem=dma((2, self.tensors)),
            fwd_sem=dma((2, self.tensors)),
            back_sum_sem=dma((2,)),
            gp_sum_sem=dma((2,)),
            ug_sem=dma((2,)),
            ug_dp_sem=dma((2, self.dps)),
            dg_dp_sem=dma((2, self.dps)),
            act_sem=dma((2, self.chunks)),
        )

    def __call__(self, blocks, pads, tenant, table, act, grad, q, kv, saved, down, up, acts, gd, gu, **v):
        self.__dict__.update(v)
        self.meta = (blocks, pads, tenant, table)
        n, w, rank = self.length, self.width, self.rank
        me = {a: lax.axis_index(a) for a in ("section", "tensor", "dp")}

        def device(section=0, tensor=0, dp=0):
            return {
                "section": lax.rem(me["section"] + section + self.sections, self.sections),
                "tensor": lax.rem(me["tensor"] + tensor, self.tensors),
                "dp": lax.rem(me["dp"] + dp, self.dps),
            }

        def send(source, target, sems, where):
            return pltpu.make_async_remote_copy(
                src_ref=source,
                dst_ref=target,
                send_sem=sems[0],
                recv_sem=sems[1],
                device_id=where,
                device_id_type=pl.DeviceIdType.MESH,
            )

        def pair(sem, k):
            return sem.at[0, k], sem.at[1, k]

        def act_chunk(c):
            rows = pl.ds(pl.multiple_of(c * CHUNK, CHUNK), CHUNK)
            return send(
                act.at[0, rows, :], self.arrived.at[rows, :], pair(self.act_sem, c), device(section=1)
            )

        barrier = pltpu.get_barrier_semaphore()
        partners = [device(section=s) for s in (1, -1)]
        partners += [device(tensor=k) for k in range(1, self.tensors)]
        partners += [device(dp=k) for k in range(1, self.dps)]
        for partner in partners:
            pl.semaphore_signal(
                barrier, inc=1, device_id=partner, device_id_type=pl.DeviceIdType.MESH
            )

        loads = [
            pltpu.make_async_copy(source, target, self.load_sem.at[i])
            for i, (source, target) in enumerate(
                (
                    (up.at[0], self.up_v),
                    (saved.at[0], self.saved_v),
                    (down.at[0], self.down_v),
                    (kv.at[0], self.kv_v),
                    (q.at[0], self.q_v),
                    (grad.at[0], self.grad_v),
                )
            )
        ]
        for load in loads:
            load.start()

        tokens = token_row(n)
        bounds = seg_bounds(blocks, pads, 1)
        slots = seg_slots(tenant, table, 1)
        alive = tokens < by_segment(tokens, bounds, [b[2] for b in bounds])
        line = lax.broadcasted_iota(jnp.int32, (8, n), 0)
        tok = jnp.where(alive, by_segment(tokens, bounds, list(range(self.segs))), -1) + 0 * line
        for i, slot in enumerate(slots):
            tok = jnp.where(line == i + 1, slot, tok)
        self.tok[...] = tok
        back_slot = by_segment(tokens, bounds, slots)

        loads[0].wait()
        for i, slot in enumerate(slots):
            self.up_send[i * rank : (i + 1) * rank, :] = self.up_v[slot]
        pl.semaphore_wait(barrier, len(partners))
        act_chunk(0).start()

        sent = []

        def start(copy):
            copy.start()
            sent.append(copy)
            return copy

        def to_tensor(part, source, target, sem):
            source[...] = part
            return [
                start(send(source, target.at[k], pair(sem, k), device(tensor=k)))
                for k in range(1, self.tensors)
            ]

        def tensor_sum(copies, source, target):
            for copy in copies:
                copy.wait_recv()
            return source[...] + sum(target[k] for k in range(1, self.tensors))

        up_copy = start(send(self.up_send, self.up_in, (self.up_sem.at[0], self.up_sem.at[1]), device(section=1)))
        tok_copy = start(send(self.tok, self.tok_in, (self.tok_sem.at[0], self.tok_sem.at[1]), device(section=1)))
        tok_dp_copies = [
            start(send(self.tok, self.tok_dp.at[k], pair(self.tok_dp_sem, k), device(dp=k)))
            for k in range(1, self.dps)
        ]

        loads[1].wait()
        loads[2].wait()
        self.acc[...] = jnp.zeros_like(self.acc)

        @pl.loop(0, w // COLS)
        def _(i):
            cols = pl.ds(pl.multiple_of(i * COLS, COLS), COLS)
            right = self.down_v[:, :, cols].reshape(self.rows, COLS)
            self.acc[...] += dot(self.saved_v[:, cols], right, (1, 1))

        back_part = select_rows(self.acc[...].T, range(self.slots), back_slot, rank)
        back_copies = to_tensor(back_part, self.back_send, self.back_in, self.back_sem)
        act_chunk(1).start()

        loads[3].wait()
        loads[4].wait()
        self.prepare_attention()
        self.acc[...] = jnp.zeros_like(self.acc)
        few = max(1, self.steps // 8)
        early, late = self.steps * 3 // 8, self.steps * 7 // 8

        def attend_steps(first, last):
            @pl.loop(first, last)
            def _(step):
                self.attend(step)
                act_chunk(2 + step).start()

        attend_steps(0, few)
        self.back_sum[...] = tensor_sum(back_copies, self.back_send, self.back_in).astype(BF16)
        back_copy = start(
            send(self.back_sum, self.back_there, (self.back_sum_sem.at[0], self.back_sum_sem.at[1]), device(section=1))
        )
        attend_steps(few, early)

        loads[5].wait()
        up_copy.wait_recv()
        tok_copy.wait_recv()
        back_copy.wait_recv()
        seg_row = self.tok_in[0:1, :]
        total = self.back_there[...].astype(F32)
        spread = spread_rows(total, range(self.segs), seg_row).astype(BF16)
        fill = jnp.zeros((self.rows - self.packed, COLS), BF16)
        full = jnp.zeros((n, self.rows), F32)
        for i in range(w // COLS):
            cols = slice(i * COLS, (i + 1) * COLS)
            block = self.grad_v[:, cols]
            full = full + dot(block, jnp.concatenate([self.up_in[:, cols], fill], axis=0), (1, 1))
            self.ug_send[:, cols] = (SCALE * dot(spread, block, (1, 0))).astype(BF16)
        gp_part = select_rows(full.T, range(self.segs), seg_row, rank)
        gp_copies = to_tensor(gp_part, self.gp_send, self.gp_in, self.gp_sem)
        ug_copy = start(send(self.ug_send, self.ug_dp.at[0], (self.ug_sem.at[0], self.ug_sem.at[1]), device(section=-1)))

        attend_steps(early, early + few)
        total = tensor_sum(gp_copies, self.gp_send, self.gp_in)
        self.gp_sum[...] = (SCALE * total).astype(BF16)
        gp_copy = start(
            send(self.gp_sum, self.gp_there, (self.gp_sum_sem.at[0], self.gp_sum_sem.at[1]), device(section=-1))
        )
        attend_steps(early + few, late)

        ug_copy.wait_recv()
        ug_dp_copies = [
            start(send(self.ug_dp.at[0], self.ug_dp.at[k], pair(self.ug_dp_sem, k), device(dp=k)))
            for k in range(1, self.dps)
        ]
        gp_copy.wait_recv()
        total = self.gp_there[...].astype(F32)
        spread = spread_rows(total, range(self.segs), self.tok[0:1, :]).astype(BF16)
        for i in range(w // COLS):
            cols = slice(i * COLS, (i + 1) * COLS)
            self.dg_dp[0, :, cols] = dot(spread, self.saved_v[:, cols], (1, 0)).astype(BF16)
        dg_dp_copies = [
            start(send(self.dg_dp.at[0], self.dg_dp.at[k], pair(self.dg_dp_sem, k), device(dp=k)))
            for k in range(1, self.dps)
        ]

        attend_steps(late, self.steps)

        bounds = seg_bounds(blocks, pads, 0)
        fwd_slot = by_segment(tokens, bounds, seg_slots(tenant, table, 0))
        fwd_part = select_rows(self.acc[...].T, range(self.slots), fwd_slot, rank)
        fwd_copies = to_tensor(fwd_part, self.fwd_send, self.fwd_in, self.fwd_sem)
        total = tensor_sum(fwd_copies, self.fwd_send, self.fwd_in).astype(BF16).astype(F32)
        spread = spread_rows(total, range(self.slots), fwd_slot).T.astype(BF16)
        for i in range(w // COLS):
            cols = slice(i * COLS, (i + 1) * COLS)
            right = self.up_v[:, :, cols].reshape(self.rows, COLS)
            self.update[:, cols] = SCALE * dot(spread, right, (1, 0))

        issued = 2 + self.steps

        def acts_out(c):
            rows = pl.ds(pl.multiple_of(c * CHUNK, CHUNK), CHUNK)
            return pltpu.make_async_copy(self.acts_v.at[rows, :], acts.at[0, rows, :], self.acts_sem.at[c])

        def add_chunks(first, last):
            @pl.loop(first, last)
            def _(c):
                @pl.when(c + issued < self.chunks)
                def _():
                    act_chunk(c + issued).start()

                act_chunk(c).wait_recv()
                rows = pl.ds(pl.multiple_of(c * CHUNK, CHUNK), CHUNK)
                added = self.arrived[rows, :].astype(F32) + self.update[rows, :]
                self.acts_v[rows, :] = added.astype(BF16)
                acts_out(c).start()

        before = self.chunks * 3 // 4
        add_chunks(0, before)
        for copy in tok_dp_copies + ug_dp_copies + dg_dp_copies:
            copy.wait_recv()
        self.tok_dp[0] = self.tok[...]
        self.place(self.dg_dp, self.gd_v, me["dp"])
        self.place(self.ug_dp, self.gu_v, me["dp"])
        stores = [
            pltpu.make_async_copy(self.gd_v, gd.at[0], self.store_sem.at[0]),
            pltpu.make_async_copy(self.gu_v, gu.at[0], self.store_sem.at[1]),
        ]
        for store in stores:
            store.start()
        add_chunks(before, self.chunks)

        for store in stores:
            store.wait()
        for copy in sent:
            copy.wait_send()

        @pl.loop(0, self.chunks)
        def _(c):
            act_chunk(c).wait_send()
            acts_out(c).wait()

    def window(self, tile):
        return max(0, tile * TILE - MAX_SEG), (tile + 1) * TILE

    def prepare_attention(self):
        blocks, pads = self.meta[:2]
        bounds = seg_bounds(blocks, pads, 0)
        for head in range(self.kv_heads):
            self.v_ones[head, :, :HD] = self.kv_v[1, :, head * HD : (head + 1) * HD]
            self.v_ones[head, :, HD:] = jnp.ones((self.length, HD), BF16)
        for tile in range(self.length // TILE):
            first, last = self.window(tile)
            here = slice(tile * TILE, (tile + 1) * TILE)
            rows = tile * TILE + lax.broadcasted_iota(jnp.int32, (TILE, last - first), 0)
            cols = first + lax.broadcasted_iota(jnp.int32, (TILE, last - first), 1)
            starts = by_segment(rows, bounds, [b[0] for b in bounds])
            ends = by_segment(rows, bounds, [b[2] for b in bounds])
            seen = (cols >= starts) & (cols <= rows) & (cols < ends)
            self.bias[here, : last - first] = jnp.where(seen, 0.0, -1e30)
            rows = tile * TILE + lax.broadcasted_iota(jnp.int32, (TILE, HD), 0)
            ends = by_segment(rows, bounds, [b[2] for b in bounds])
            self.live[here, :] = jnp.where(rows < ends, 1.0, 0.0)

    def attend(self, step):
        factor = math.log2(math.e) / math.sqrt(HD)
        span = STEP_HEADS * HD
        base = pl.multiple_of(step * span, span)
        head = step // self.steps_per_kv
        key_cols = pl.ds(pl.multiple_of(head * HD, HD), HD)
        for tile in range(self.length // TILE):
            first, last = self.window(tile)
            here = slice(tile * TILE, (tile + 1) * TILE)
            block = self.q_v[here, pl.ds(base, span)]
            for two in range(0, STEP_HEADS, 2):
                queries = jnp.concatenate(
                    [block[:, h * HD : (h + 1) * HD] for h in (two, two + 1)], axis=0
                )
                scores = dot(queries, self.kv_v[0, first:last, key_cols], (1, 1))
                scores = scores.reshape(2, TILE, last - first)
                scores = scores * factor + self.bias[here, : last - first][None]
                top = jnp.max(scores, axis=-1, keepdims=True)
                weights = jnp.exp2(scores - top).astype(BF16).reshape(2 * TILE, last - first)
                mixed = dot(weights, self.v_ones[head, first:last, :], (1, 0))
                for i, h in enumerate((two, two + 1)):
                    part = mixed[i * TILE : (i + 1) * TILE]
                    value = part[:, :HD] * (self.live[here, :] / part[:, HD:])
                    self.att[here, h * HD : (h + 1) * HD] = value.astype(BF16)
        right = self.down_v[:, :, pl.ds(base, span)].reshape(self.rows, span)
        self.acc[...] += dot(self.att[...], right, (1, 1))

    def place(self, compact, out, my_dp):
        rank, n = self.rank, self.length

        @pl.loop(0, self.width // n)
        def _(i):
            cols = pl.ds(pl.multiple_of(i * n, n), n)
            totals = [jnp.zeros((rank, n), F32)] * self.slots
            for d in range(self.dps):
                k = lax.rem(my_dp - d + self.dps, self.dps)
                for s in range(self.segs):
                    key = self.tok_dp[k, s + 1 : s + 2, :]
                    rows = compact[k, s * rank : (s + 1) * rank, cols].astype(F32)
                    for slot in range(self.slots):
                        totals[slot] = totals[slot] + jnp.where(key == slot, rows, 0.0)
            for slot in range(self.slots):
                out[slot, :, cols] = totals[slot].astype(BF16)


def per_device(sizes, act, grad, queries, keys_values, saved, down, up, blocks, pads, tenant, table):
    kernel = Kernel(sizes, (queries.shape, keys_values.shape[-1], up.shape, blocks.shape[-1]))
    scratch = kernel.scratch()
    names = list(scratch)

    def body(*refs):
        kernel(*refs[: -len(names)], **dict(zip(names, refs[-len(names) :])))

    held = (
        pl.pallas_call(
            body,
            out_shape=[pltpu.VMEM(a.shape, BF16) for a in (act, down, up)],
            in_specs=[SMEM] * 4 + [pl.BlockSpec(memory_space=pl.ANY)] * 7,
            out_specs=[pl.BlockSpec(memory_space=pl.ANY)] * 3,
            scratch_shapes=list(scratch.values()),
            compiler_params=pltpu.CompilerParams(
                vmem_limit_bytes=VMEM_BYTES, collective_id=0, has_side_effects=True
            ),
            name="adapter_step",
        )(
            blocks,
            pads,
            tenant,
            table,
            *[
                pltpu.with_memory_space_constraint(a, pltpu.HBM)
                for a in (act, grad, queries, keys_values, saved, down, up)
            ],
        )
    )
    return tuple(
        pl.pallas_call(
            write_kernel,
            out_shape=[jax.ShapeDtypeStruct(a.shape, BF16) for a in held],
            in_specs=[pl.BlockSpec(memory_space=pl.ANY)] * 3,
            out_specs=[pl.BlockSpec(memory_space=pl.ANY)] * 3,
            scratch_shapes=[pltpu.SemaphoreType.DMA((WRITES + 2,))],
            compiler_params=pltpu.CompilerParams(vmem_limit_bytes=2 * 1024 * 1024),
            name="write_results",
        )(*[pltpu.with_memory_space_constraint(a, pltpu.VMEM) for a in held])
    )


def write_kernel(acts_v, gd_v, gu_v, acts, gd, gu, sem):
    rows = acts.shape[1] // WRITES
    copies = [
        pltpu.make_async_copy(
            acts_v.at[0, i * rows : (i + 1) * rows], acts.at[0, i * rows : (i + 1) * rows], sem.at[i]
        )
        for i in range(WRITES)
    ]
    copies.append(pltpu.make_async_copy(gd_v, gd, sem.at[WRITES]))
    copies.append(pltpu.make_async_copy(gu_v, gu, sem.at[WRITES + 1]))
    for copy in copies:
        copy.start()
    for copy in copies:
        copy.wait()


def solution(mesh):
    wide = P("section", "dp", "tensor")
    adapter = P("section", None, None, "tensor")
    per_segment = P("section", None, "dp", None)
    return jax.shard_map(
        functools.partial(per_device, dict(mesh.shape)),
        mesh=mesh,
        in_specs=(
            wide,
            wide,
            wide,
            P("section", None, "dp", "tensor"),
            wide,
            adapter,
            adapter,
            per_segment,
            per_segment,
            per_segment,
            P(),
        ),
        out_specs=(wide, adapter, adapter),
        check_vma=False,
    )
```

```python
import functools
import math

import jax
import jax.numpy as jnp
from jax import lax
from jax.experimental import pallas as pl
from jax.experimental.pallas import tpu as pltpu
from jax.sharding import PartitionSpec as P

HD = 128
BLOCK = 64
MAX_SEG = 4 * BLOCK
TILE = 128
SCALE = 2.0
F32 = jnp.float32
BF16 = jnp.bfloat16
VMEM_BYTES = 50 * 1024 * 1024
CHUNK = 32
COLS = 1024
STEP_HEADS = 4
WRITES = 4

SMEM = pl.BlockSpec(memory_space=pltpu.SMEM)


def dot(left, right, dims):
    return lax.dot_general(left, right, ((dims[:1], dims[1:]), ((), ())), preferred_element_type=F32)


def seg_bounds(blocks, pads, batch):
    bounds, start = [], 0
    for i in range(blocks.shape[-1]):
        end = start + blocks[0, batch, 0, i] * BLOCK
        bounds.append((start, end, end - pads[0, batch, 0, i]))
        start = end
    return bounds


def seg_slots(tenant, table, batch):
    return [table[tenant[0, batch, 0, i]] for i in range(tenant.shape[-1])]


def by_segment(pos, bounds, values):
    out = jnp.zeros_like(pos) + values[0]
    for (start, _, _), value in zip(bounds[1:], values[1:]):
        out = jnp.where(pos >= start, value, out)
    return out


def select_rows(full, keys, key_row, rank):
    out = jnp.zeros((rank, full.shape[1]), F32)
    for i, key in enumerate(keys):
        out = out + jnp.where(key_row == key, full[i * rank : (i + 1) * rank], 0.0)
    return out


def spread_rows(ranked, keys, key_row):
    return jnp.concatenate([jnp.where(key_row == key, ranked, 0.0) for key in keys], axis=0)


def token_row(length):
    return lax.broadcasted_iota(jnp.int32, (1, length), 1)


class Kernel:
    def __init__(self, sizes, shapes):
        self.sections, self.tensors, self.dps = sizes["section"], sizes["tensor"], sizes["dp"]
        (_, self.length, self.width), self.kv_width, (_, self.slots, self.rank, _), self.segs = shapes
        self.rows = self.slots * self.rank
        self.packed = self.segs * self.rank
        self.kv_heads = self.kv_width // HD
        self.steps = self.width // (STEP_HEADS * HD)
        self.steps_per_kv = self.steps // self.kv_heads
        self.chunks = self.length // CHUNK

    def scratch(self):
        n, w, r, p = self.length, self.width, self.rank, self.packed
        dma = pltpu.SemaphoreType.DMA
        wide = pltpu.VMEM((n, w), BF16)
        adapter = pltpu.VMEM((self.slots, r, w), BF16)
        ranks = pltpu.VMEM((self.tensors, r, n), F32)
        one = pltpu.VMEM((r, n), F32)
        half = pltpu.VMEM((r, n), BF16)
        return dict(
            up_v=adapter,
            down_v=adapter,
            saved_v=wide,
            grad_v=wide,
            q_v=wide,
            kv_v=pltpu.VMEM((2, n, self.kv_width), BF16),
            up_send=pltpu.VMEM((p, w), BF16),
            up_in=pltpu.VMEM((p, w), BF16),
            tok=pltpu.VMEM((8, n), jnp.int32),
            tok_in=pltpu.VMEM((8, n), jnp.int32),
            tok_dp=pltpu.VMEM((self.dps, 8, n), jnp.int32),
            back_send=one,
            back_in=ranks,
            back_sum=half,
            back_there=half,
            gp_send=one,
            gp_in=ranks,
            gp_sum=half,
            gp_there=half,
            fwd_send=one,
            fwd_in=ranks,
            ug_send=pltpu.VMEM((p, w), BF16),
            ug_dp=pltpu.VMEM((self.dps, p, w), BF16),
            dg_dp=pltpu.VMEM((self.dps, p, w), BF16),
            arrived=wide,
            update=pltpu.VMEM((n, w), F32),
            acts_v=wide,
            gd_v=adapter,
            gu_v=adapter,
            acc=pltpu.VMEM((n, self.rows), F32),
            bias=pltpu.VMEM((n, MAX_SEG + TILE), F32),
            live=pltpu.VMEM((n, HD), F32),
            v_ones=pltpu.VMEM((self.kv_heads, n, 2 * HD), BF16),
            att=pltpu.VMEM((n, STEP_HEADS * HD), BF16),
            load_sem=dma((6,)),
            store_sem=dma((2,)),
            acts_sem=dma((self.chunks,)),
            up_sem=dma((2,)),
            tok_sem=dma((2,)),
            tok_dp_sem=dma((2, self.dps)),
            back_sem=dma((2, self.tensors)),
            gp_sem=dma((2, self.tensors)),
            fwd_sem=dma((2, self.tensors)),
            back_sum_sem=dma((2,)),
            gp_sum_sem=dma((2,)),
            ug_sem=dma((2,)),
            ug_dp_sem=dma((2, self.dps)),
            dg_dp_sem=dma((2, self.dps)),
            act_sem=dma((2, self.chunks)),
        )

    def __call__(self, blocks, pads, tenant, table, act, grad, q, kv, saved, down, up, acts, gd, gu, **v):
        self.__dict__.update(v)
        self.meta = (blocks, pads, tenant, table)
        n, w, rank = self.length, self.width, self.rank
        me = {a: lax.axis_index(a) for a in ("section", "tensor", "dp")}

        def device(section=0, tensor=0, dp=0):
            return {
                "section": lax.rem(me["section"] + section + self.sections, self.sections),
                "tensor": lax.rem(me["tensor"] + tensor, self.tensors),
                "dp": lax.rem(me["dp"] + dp, self.dps),
            }

        def send(source, target, sems, where):
            return pltpu.make_async_remote_copy(
                src_ref=source,
                dst_ref=target,
                send_sem=sems[0],
                recv_sem=sems[1],
                device_id=where,
                device_id_type=pl.DeviceIdType.MESH,
            )

        def pair(sem, k):
            return sem.at[0, k], sem.at[1, k]

        def act_chunk(c):
            rows = pl.ds(pl.multiple_of(c * CHUNK, CHUNK), CHUNK)
            return send(
                act.at[0, rows, :], self.arrived.at[rows, :], pair(self.act_sem, c), device(section=1)
            )

        barrier = pltpu.get_barrier_semaphore()
        partners = [device(section=s) for s in (1, -1)]
        partners += [device(tensor=k) for k in range(1, self.tensors)]
        partners += [device(dp=k) for k in range(1, self.dps)]
        for partner in partners:
            pl.semaphore_signal(
                barrier, inc=1, device_id=partner, device_id_type=pl.DeviceIdType.MESH
            )

        loads = [
            pltpu.make_async_copy(source, target, self.load_sem.at[i])
            for i, (source, target) in enumerate(
                (
                    (up.at[0], self.up_v),
                    (saved.at[0], self.saved_v),
                    (down.at[0], self.down_v),
                    (kv.at[0], self.kv_v),
                    (q.at[0], self.q_v),
                    (grad.at[0], self.grad_v),
                )
            )
        ]
        for load in loads:
            load.start()

        tokens = token_row(n)
        bounds = seg_bounds(blocks, pads, 1)
        slots = seg_slots(tenant, table, 1)
        alive = tokens < by_segment(tokens, bounds, [b[2] for b in bounds])
        line = lax.broadcasted_iota(jnp.int32, (8, n), 0)
        tok = jnp.where(alive, by_segment(tokens, bounds, list(range(self.segs))), -1) + 0 * line
        for i, slot in enumerate(slots):
            tok = jnp.where(line == i + 1, slot, tok)
        self.tok[...] = tok
        back_slot = by_segment(tokens, bounds, slots)

        loads[0].wait()
        for i, slot in enumerate(slots):
            self.up_send[i * rank : (i + 1) * rank, :] = self.up_v[slot]
        pl.semaphore_wait(barrier, len(partners))
        act_chunk(0).start()

        sent = []

        def start(copy):
            copy.start()
            sent.append(copy)
            return copy

        def to_tensor(part, source, target, sem):
            source[...] = part
            return [
                start(send(source, target.at[k], pair(sem, k), device(tensor=k)))
                for k in range(1, self.tensors)
            ]

        def tensor_sum(copies, source, target):
            for copy in copies:
                copy.wait_recv()
            return source[...] + sum(target[k] for k in range(1, self.tensors))

        up_copy = start(send(self.up_send, self.up_in, (self.up_sem.at[0], self.up_sem.at[1]), device(section=1)))
        tok_copy = start(send(self.tok, self.tok_in, (self.tok_sem.at[0], self.tok_sem.at[1]), device(section=1)))
        tok_dp_copies = [
            start(send(self.tok, self.tok_dp.at[k], pair(self.tok_dp_sem, k), device(dp=k)))
            for k in range(1, self.dps)
        ]

        loads[1].wait()
        loads[2].wait()
        self.acc[...] = jnp.zeros_like(self.acc)

        @pl.loop(0, w // COLS)
        def _(i):
            cols = pl.ds(pl.multiple_of(i * COLS, COLS), COLS)
            right = self.down_v[:, :, cols].reshape(self.rows, COLS)
            self.acc[...] += dot(self.saved_v[:, cols], right, (1, 1))

        back_part = select_rows(self.acc[...].T, range(self.slots), back_slot, rank)
        back_copies = to_tensor(back_part, self.back_send, self.back_in, self.back_sem)
        act_chunk(1).start()

        loads[3].wait()
        loads[4].wait()
        self.prepare_attention()
        self.acc[...] = jnp.zeros_like(self.acc)
        few = max(1, self.steps // 8)
        early, late = self.steps * 3 // 8, self.steps * 7 // 8

        def attend_steps(first, last, ahead):
            @pl.loop(first, last)
            def _(step):
                self.attend(step)
                act_chunk(ahead + step).start()

        attend_steps(0, few, 2)
        self.back_sum[...] = tensor_sum(back_copies, self.back_send, self.back_in).astype(BF16)
        back_copy = start(
            send(self.back_sum, self.back_there, (self.back_sum_sem.at[0], self.back_sum_sem.at[1]), device(section=1))
        )
        act_chunk(few + 2).start()
        attend_steps(few, early, 3)
        act_chunk(early + 3).start()

        loads[5].wait()
        up_copy.wait_recv()
        tok_copy.wait_recv()
        back_copy.wait_recv()
        seg_row = self.tok_in[0:1, :]
        total = self.back_there[...].astype(F32)
        spread = spread_rows(total, range(self.segs), seg_row).astype(BF16)
        fill = jnp.zeros((self.rows - self.packed, COLS), BF16)
        full = jnp.zeros((n, self.rows), F32)
        for i in range(w // COLS):
            cols = slice(i * COLS, (i + 1) * COLS)
            block = self.grad_v[:, cols]
            full = full + dot(block, jnp.concatenate([self.up_in[:, cols], fill], axis=0), (1, 1))
            self.ug_send[:, cols] = (SCALE * dot(spread, block, (1, 0))).astype(BF16)
        gp_part = select_rows(full.T, range(self.segs), seg_row, rank)
        gp_copies = to_tensor(gp_part, self.gp_send, self.gp_in, self.gp_sem)
        ug_copy = start(send(self.ug_send, self.ug_dp.at[0], (self.ug_sem.at[0], self.ug_sem.at[1]), device(section=-1)))

        attend_steps(early, early + few, 4)
        total = tensor_sum(gp_copies, self.gp_send, self.gp_in)
        self.gp_sum[...] = (SCALE * total).astype(BF16)
        gp_copy = start(
            send(self.gp_sum, self.gp_there, (self.gp_sum_sem.at[0], self.gp_sum_sem.at[1]), device(section=-1))
        )
        attend_steps(early + few, late, 4)

        ug_copy.wait_recv()
        ug_dp_copies = [
            start(send(self.ug_dp.at[0], self.ug_dp.at[k], pair(self.ug_dp_sem, k), device(dp=k)))
            for k in range(1, self.dps)
        ]
        gp_copy.wait_recv()
        total = self.gp_there[...].astype(F32)
        spread = spread_rows(total, range(self.segs), self.tok[0:1, :]).astype(BF16)
        for i in range(w // COLS):
            cols = slice(i * COLS, (i + 1) * COLS)
            self.dg_dp[0, :, cols] = dot(spread, self.saved_v[:, cols], (1, 0)).astype(BF16)
        dg_dp_copies = [
            start(send(self.dg_dp.at[0], self.dg_dp.at[k], pair(self.dg_dp_sem, k), device(dp=k)))
            for k in range(1, self.dps)
        ]

        attend_steps(late, self.steps, 4)

        bounds = seg_bounds(blocks, pads, 0)
        fwd_slot = by_segment(tokens, bounds, seg_slots(tenant, table, 0))
        fwd_part = select_rows(self.acc[...].T, range(self.slots), fwd_slot, rank)
        fwd_copies = to_tensor(fwd_part, self.fwd_send, self.fwd_in, self.fwd_sem)
        total = tensor_sum(fwd_copies, self.fwd_send, self.fwd_in).astype(BF16).astype(F32)
        spread = spread_rows(total, range(self.slots), fwd_slot).T.astype(BF16)
        for i in range(w // COLS):
            cols = slice(i * COLS, (i + 1) * COLS)
            right = self.up_v[:, :, cols].reshape(self.rows, COLS)
            self.update[:, cols] = SCALE * dot(spread, right, (1, 0))

        issued = 4 + self.steps

        def acts_out(c):
            rows = pl.ds(pl.multiple_of(c * CHUNK, CHUNK), CHUNK)
            return pltpu.make_async_copy(self.acts_v.at[rows, :], acts.at[0, rows, :], self.acts_sem.at[c])

        def add_chunks(first, last):
            @pl.loop(first, last)
            def _(c):
                @pl.when(c + issued < self.chunks)
                def _():
                    act_chunk(c + issued).start()

                act_chunk(c).wait_recv()
                rows = pl.ds(pl.multiple_of(c * CHUNK, CHUNK), CHUNK)
                added = self.arrived[rows, :].astype(F32) + self.update[rows, :]
                self.acts_v[rows, :] = added.astype(BF16)
                acts_out(c).start()

        before = self.chunks * 3 // 4
        add_chunks(0, before)
        for copy in tok_dp_copies + ug_dp_copies + dg_dp_copies:
            copy.wait_recv()
        self.tok_dp[0] = self.tok[...]
        self.place(self.dg_dp, self.gd_v, me["dp"])
        self.place(self.ug_dp, self.gu_v, me["dp"])
        stores = [
            pltpu.make_async_copy(self.gd_v, gd.at[0], self.store_sem.at[0]),
            pltpu.make_async_copy(self.gu_v, gu.at[0], self.store_sem.at[1]),
        ]
        for store in stores:
            store.start()
        add_chunks(before, self.chunks)

        for store in stores:
            store.wait()
        for copy in sent:
            copy.wait_send()

        @pl.loop(0, self.chunks)
        def _(c):
            act_chunk(c).wait_send()
            acts_out(c).wait()

    def window(self, tile):
        return max(0, tile * TILE - MAX_SEG), (tile + 1) * TILE

    def prepare_attention(self):
        blocks, pads = self.meta[:2]
        bounds = seg_bounds(blocks, pads, 0)
        for head in range(self.kv_heads):
            self.v_ones[head, :, :HD] = self.kv_v[1, :, head * HD : (head + 1) * HD]
            self.v_ones[head, :, HD:] = jnp.ones((self.length, HD), BF16)
        for tile in range(self.length // TILE):
            first, last = self.window(tile)
            here = slice(tile * TILE, (tile + 1) * TILE)
            rows = tile * TILE + lax.broadcasted_iota(jnp.int32, (TILE, last - first), 0)
            cols = first + lax.broadcasted_iota(jnp.int32, (TILE, last - first), 1)
            starts = by_segment(rows, bounds, [b[0] for b in bounds])
            ends = by_segment(rows, bounds, [b[2] for b in bounds])
            seen = (cols >= starts) & (cols <= rows) & (cols < ends)
            self.bias[here, : last - first] = jnp.where(seen, 0.0, -1e30)
            rows = tile * TILE + lax.broadcasted_iota(jnp.int32, (TILE, HD), 0)
            ends = by_segment(rows, bounds, [b[2] for b in bounds])
            self.live[here, :] = jnp.where(rows < ends, 1.0, 0.0)

    def attend(self, step):
        factor = math.log2(math.e) / math.sqrt(HD)
        span = STEP_HEADS * HD
        base = pl.multiple_of(step * span, span)
        head = step // self.steps_per_kv
        key_cols = pl.ds(pl.multiple_of(head * HD, HD), HD)
        for tile in range(self.length // TILE):
            first, last = self.window(tile)
            here = slice(tile * TILE, (tile + 1) * TILE)
            block = self.q_v[here, pl.ds(base, span)]
            for two in range(0, STEP_HEADS, 2):
                queries = jnp.concatenate(
                    [block[:, h * HD : (h + 1) * HD] for h in (two, two + 1)], axis=0
                )
                scores = dot(queries, self.kv_v[0, first:last, key_cols], (1, 1))
                scores = scores.reshape(2, TILE, last - first)
                scores = scores * factor + self.bias[here, : last - first][None]
                top = jnp.max(scores, axis=-1, keepdims=True)
                weights = jnp.exp2(scores - top).astype(BF16).reshape(2 * TILE, last - first)
                mixed = dot(weights, self.v_ones[head, first:last, :], (1, 0))
                for i, h in enumerate((two, two + 1)):
                    part = mixed[i * TILE : (i + 1) * TILE]
                    value = part[:, :HD] * (self.live[here, :] / part[:, HD:])
                    self.att[here, h * HD : (h + 1) * HD] = value.astype(BF16)
        right = self.down_v[:, :, pl.ds(base, span)].reshape(self.rows, span)
        self.acc[...] += dot(self.att[...], right, (1, 1))

    def place(self, compact, out, my_dp):
        rank, n = self.rank, self.length

        @pl.loop(0, self.width // n)
        def _(i):
            cols = pl.ds(pl.multiple_of(i * n, n), n)
            totals = [jnp.zeros((rank, n), F32)] * self.slots
            for d in range(self.dps):
                k = lax.rem(my_dp - d + self.dps, self.dps)
                for s in range(self.segs):
                    key = self.tok_dp[k, s + 1 : s + 2, :]
                    rows = compact[k, s * rank : (s + 1) * rank, cols].astype(F32)
                    for slot in range(self.slots):
                        totals[slot] = totals[slot] + jnp.where(key == slot, rows, 0.0)
            for slot in range(self.slots):
                out[slot, :, cols] = totals[slot].astype(BF16)


def per_device(sizes, act, grad, queries, keys_values, saved, down, up, blocks, pads, tenant, table):
    kernel = Kernel(sizes, (queries.shape, keys_values.shape[-1], up.shape, blocks.shape[-1]))
    scratch = kernel.scratch()
    names = list(scratch)

    def body(*refs):
        kernel(*refs[: -len(names)], **dict(zip(names, refs[-len(names) :])))

    held = (
        pl.pallas_call(
            body,
            out_shape=[pltpu.VMEM(a.shape, BF16) for a in (act, down, up)],
            in_specs=[SMEM] * 4 + [pl.BlockSpec(memory_space=pl.ANY)] * 7,
            out_specs=[pl.BlockSpec(memory_space=pl.ANY)] * 3,
            scratch_shapes=list(scratch.values()),
            compiler_params=pltpu.CompilerParams(
                vmem_limit_bytes=VMEM_BYTES, collective_id=0, has_side_effects=True
            ),
            name="adapter_step",
        )(
            blocks,
            pads,
            tenant,
            table,
            *[
                pltpu.with_memory_space_constraint(a, pltpu.HBM)
                for a in (act, grad, queries, keys_values, saved, down, up)
            ],
        )
    )
    return tuple(
        pl.pallas_call(
            write_kernel,
            out_shape=[jax.ShapeDtypeStruct(a.shape, BF16) for a in held],
            in_specs=[pl.BlockSpec(memory_space=pl.ANY)] * 3,
            out_specs=[pl.BlockSpec(memory_space=pl.ANY)] * 3,
            scratch_shapes=[pltpu.SemaphoreType.DMA((WRITES + 2,))],
            compiler_params=pltpu.CompilerParams(vmem_limit_bytes=2 * 1024 * 1024),
            name="write_results",
        )(*[pltpu.with_memory_space_constraint(a, pltpu.VMEM) for a in held])
    )


def write_kernel(acts_v, gd_v, gu_v, acts, gd, gu, sem):
    rows = acts.shape[1] // WRITES
    copies = [
        pltpu.make_async_copy(
            acts_v.at[0, i * rows : (i + 1) * rows], acts.at[0, i * rows : (i + 1) * rows], sem.at[i]
        )
        for i in range(WRITES)
    ]
    copies.append(pltpu.make_async_copy(gd_v, gd, sem.at[WRITES]))
    copies.append(pltpu.make_async_copy(gu_v, gu, sem.at[WRITES + 1]))
    for copy in copies:
        copy.start()
    for copy in copies:
        copy.wait()


def solution(mesh):
    wide = P("section", "dp", "tensor")
    adapter = P("section", None, None, "tensor")
    per_segment = P("section", None, "dp", None)
    return jax.shard_map(
        functools.partial(per_device, dict(mesh.shape)),
        mesh=mesh,
        in_specs=(
            wide,
            wide,
            wide,
            P("section", None, "dp", "tensor"),
            wide,
            adapter,
            adapter,
            per_segment,
            per_segment,
            per_segment,
            P(),
        ),
        out_specs=(wide, adapter, adapter),
        check_vma=False,
    )
```
